512 devices in a mesh: dp: 64 (over z, y), context: 8 (over x, core).
Axes of the slice: x: 4, y: 4, z: 16, core: 2. Of those that a mesh axis runs over, the one named last changes fastest.
Arguments:
- hidden_in: bfloat16 [64, 1024, 2048], P('dp', 'context'), may hold values from -6 to 6
- cotangent: bfloat16 [64, 1024, 2048], P('dp', 'context'), may hold values from -6 to 6
- tile_depth: int32 [64, 8], P('dp'), may hold values from 1 to 4, as said below
- w_qkv: bfloat16 [3, 2048, 1024], P(None, 'dp', 'context'), may hold values from -0.125 to 0.125
- w_out: bfloat16 [1024, 2048], P('context', 'dp'), may hold values from -0.1875 to 0.1875
- gain: float32 [2048], replicated, may hold values from 0.1 to 1.9
Outputs:
- hidden_out: bfloat16 [64, 1024, 2048], P('dp', 'context')
- grad_in: bfloat16 [64, 1024, 2048], P('dp', 'context')
- grad_qkv: float32 [3, 2048, 1024], P(None, 'dp', 'context')
- grad_out: float32 [1024, 2048], P('context', 'dp')
The draws below stay inside these ranges and needn't reach their ends.
Inputs may be any that keep to these rules, and one draw needn't show every extreme that they name: `tile_depth`: in every document at most 1 tiles have depth 2 or more and at most 1 have depth 3 or more; some document has exactly 1 and 1 such tiles.
All inputs are finite; a program needn't handle non-finite values.
Results may differ from the reference program's by a relative error of at most 0.028.
Values may be sent and summed in bfloat16 or wider, within the bound.
No kernel may reach another device: no remote copies, remote signals or barrier semaphores. Data moves between devices by JAX's collectives and lax.ppermute only.
A program may use at most 64 MiB of HBM per device.

```python
import jax
import jax.numpy as jnp
from jax import lax

D = 2048
HD = 128
HEAD_DEV = 1
TILE = 128
HEADS = 8
INNER = 1024
TILES_DOC = 8
SEQ = 1024
DOCS = 64
CAP2 = 1
CAP3 = 1
N_CONTEXT = 8


def draw_tile_depth(key, part):
    key = jax.random.fold_in(key, 7)
    keys = jax.random.split(key, 5)
    docs = jnp.arange(DOCS)
    many2 = jax.random.randint(keys[0], (DOCS,), 0, CAP2 + 1)
    many3 = jnp.minimum(jax.random.randint(keys[1], (DOCS,), 0, CAP3 + 1), many2)
    chosen = jax.random.randint(keys[2], (), 0, DOCS)
    many2 = jnp.where(docs == chosen, CAP2, many2)
    many3 = jnp.where(docs == chosen, CAP3, many3)
    orders = jax.vmap(lambda k: jax.random.permutation(k, TILES_DOC))(jax.random.split(keys[3], DOCS))
    rank = jnp.argsort(orders, axis=-1, stable=True).astype(jnp.int32)
    extra = jax.random.randint(keys[4], (DOCS, TILES_DOC), 0, 2)
    extra = jnp.where((docs[:, None] == chosen) & (rank == 0), 1, extra)
    deep2 = (rank < many2[:, None]).astype(jnp.int32)
    deep3 = (rank < many3[:, None]).astype(jnp.int32)
    return (1 + deep2 + deep3 * (1 + extra)).astype(jnp.int32)


def shard_levels(own_key, dims, cuts, smallest, high):
    level, own = 1.0, jax.random.fold_in(own_key, 6)
    for dim, blocks in cuts:
        draws = jnp.exp(jax.random.uniform(jax.random.fold_in(own, dim), (blocks,), jnp.float32, smallest / len(cuts), high / len(cuts)))
        level = level * jnp.repeat(draws, dims[dim] // blocks).reshape([-1 if axis == dim else 1 for axis in range(len(dims))])
    return level


def bell_draw(stream_key, dims, scale, limit, cuts=(), held_as=jnp.bfloat16):
    entries = scale * jax.random.normal(stream_key, dims, jnp.float32)
    if cuts:
        entries = entries * shard_levels(stream_key, dims, cuts, -0.22, 0.18)
    return jnp.clip(entries, -limit, limit).astype(held_as)


def setup_inputs(seed: int = 0) -> dict:
    splits = jax.random.split(jax.random.key(seed), 7)
    return {
        "hidden_in": bell_draw(splits[0], (DOCS, SEQ, D), 1.0, 6.0, ((0, 64), (1, 8))),
        "cotangent": bell_draw(splits[1], (DOCS, SEQ, D), 1.0, 6.0, ((0, 64), (1, 8))),
        "tile_depth": draw_tile_depth(jax.random.fold_in(splits[6], 71), 0),
        "w_qkv": bell_draw(splits[3], (3, D, INNER), D ** -0.5, 0.125, ((1, 64), (2, 8))),
        "w_out": bell_draw(splits[4], (INNER, D), INNER ** -0.5, 0.1875, ((0, 8), (1, 64))),
        "gain": jnp.clip(1.0 + 0.18 * jax.random.normal(splits[5], (D,), jnp.float32), 0.1, 1.9),
    }


def norm_rows(x32, gain):
    inv = lax.rsqrt(lax.optimization_barrier(jnp.mean(x32 * x32, -1, keepdims=True)) + 1e-06)
    return (inv, (x32 * inv * gain).astype(jnp.bfloat16))

def slot_plan(depth, level, cap):
    alive = depth >= level
    alive_int = alive.astype(jnp.int32)
    rank = (jnp.cumsum(alive_int) - alive_int).astype(jnp.int32)
    places = jnp.arange(depth.shape[0], dtype=jnp.int32)
    owners = jnp.stack([jnp.sum(jnp.where(alive & (rank == s), places, 0)) for s in range(cap)]).astype(jnp.int32)
    valid = jnp.stack([jnp.any(alive & (rank == s)) for s in range(cap)])
    return (alive, jnp.minimum(rank, cap - 1).astype(jnp.int32), owners, valid)

def collect(tiles, owners, valid):
    picked = jnp.take(tiles, owners, axis=0)
    picked = jnp.where(valid[:, None, None], picked, jnp.zeros_like(picked))
    return picked.reshape(-1, tiles.shape[-1])

def spread(rows, rank, alive, tile):
    per_slot = rows.reshape(-1, tile, rows.shape[-1])
    back = jnp.take(per_slot, rank, axis=0)
    return jnp.where(alive[:, None, None], back, jnp.zeros_like(back))

def group_round(terms):
    rounded = lax.optimization_barrier(terms.astype(jnp.bfloat16)).astype(jnp.float32)
    return lax.optimization_barrier(jnp.sum(rounded, 0))

def doc_pass(carry, inputs):
    w_qkv, w_out, gain, acc_qkv, acc_out = carry
    hidden, grad, depth = inputs
    scale = HD ** (-0.5)
    state = hidden.reshape(N_CONTEXT, TILE, D)
    saved = []
    for level, cap in ((2, CAP2), (3, CAP3)):
        alive, rank, owners, valid = slot_plan(depth, level, cap)
        x32 = state.astype(jnp.float32)
        inv, normed = norm_rows(x32, gain)
        rows = collect(normed, owners, valid)
        count = rows.shape[0]
        qkv = jnp.einsum('rd,tdc->trc', rows.astype(jnp.float32), w_qkv.astype(jnp.float32)).astype(jnp.bfloat16)
        heads = qkv.reshape(3, count, HEADS, HD)
        query, key, value = (heads[0], heads[1], heads[2])
        valid_rows = jnp.repeat(valid, TILE)
        pos = jnp.arange(count)
        allowed = valid_rows[None, :] & (pos[None, :] <= pos[:, None])
        scores = jnp.einsum('qhd,khd->hqk', query.astype(jnp.float32), key.astype(jnp.float32)) * scale
        scores = jnp.where(allowed[None], scores, -1e+30)
        top = lax.optimization_barrier(jnp.max(scores, -1, keepdims=True))
        expo = jnp.exp(scores - top)
        prob = expo / lax.optimization_barrier(jnp.sum(expo, -1, keepdims=True))
        probb = prob.astype(jnp.bfloat16)
        attn = jnp.einsum('hqk,khd->qhd', probb.astype(jnp.float32), value.astype(jnp.float32)).astype(jnp.bfloat16)
        attn_flat = attn.reshape(count, INNER)
        groups = attn_flat.reshape(count, N_CONTEXT, HEAD_DEV * HD).astype(jnp.float32)
        w_groups = w_out.reshape(N_CONTEXT, HEAD_DEV * HD, D).astype(jnp.float32)
        mixed = group_round(jnp.einsum('rgc,gcd->grd', groups, w_groups))
        state = (x32 + spread(mixed, rank, alive, TILE)).astype(jnp.bfloat16)
        saved.append((alive, rank, owners, valid, x32, inv, rows, query, key, value, prob, probb, attn, attn_flat))
    hidden_out = state.reshape(SEQ, D)
    gstate = grad.reshape(N_CONTEXT, TILE, D)
    for index in (1, 0):
        alive, rank, owners, valid, x32, inv, rows, query, key, value, prob, probb, attn, attn_flat = saved[index]
        count = rows.shape[0]
        masked = jnp.where(alive[:, None, None], gstate, jnp.zeros_like(gstate))
        dy = collect(masked, owners, valid)
        dattn = jnp.dot(dy, w_out.T, preferred_element_type=jnp.float32).astype(jnp.bfloat16)
        acc_out = acc_out + jnp.dot(attn_flat.T, dy, preferred_element_type=jnp.float32)
        dheads = dattn.reshape(count, HEADS, HD).astype(jnp.float32)
        delta = lax.optimization_barrier(jnp.sum(dheads * attn.astype(jnp.float32), -1))
        dprob = jnp.einsum('qhd,khd->hqk', dheads, value.astype(jnp.float32))
        dscore = (prob * (dprob - delta.T[:, :, None]) * scale).astype(jnp.bfloat16).astype(jnp.float32)
        dq = jnp.einsum('hqk,khd->qhd', dscore, key.astype(jnp.float32)).astype(jnp.bfloat16)
        dk = jnp.einsum('hqk,qhd->khd', dscore, query.astype(jnp.float32)).astype(jnp.bfloat16)
        dv = jnp.einsum('hqk,qhd->khd', probb.astype(jnp.float32), dheads).astype(jnp.bfloat16)
        dqkv = jnp.stack([dq, dk, dv]).reshape(3, count, INNER).astype(jnp.float32)
        acc_qkv = acc_qkv + jnp.einsum('rd,trc->tdc', rows.astype(jnp.float32), dqkv)
        dgroups = dqkv.reshape(3, count, N_CONTEXT, HEAD_DEV * HD)
        wq_groups = w_qkv.reshape(3, D, N_CONTEXT, HEAD_DEV * HD).astype(jnp.float32)
        dnorm = group_round(jnp.einsum('trgc,tdgc->grd', dgroups, wq_groups))
        back = spread(dnorm, rank, alive, TILE)
        scaled = back * gain
        dx = inv * scaled - x32 * inv ** 3 * lax.optimization_barrier(jnp.mean(x32 * scaled, -1, keepdims=True))
        dx = jnp.where(alive[:, None, None], dx, jnp.zeros_like(dx))
        gstate = (gstate.astype(jnp.float32) + dx).astype(jnp.bfloat16)
    return ((w_qkv, w_out, gain, acc_qkv, acc_out), (hidden_out, gstate.reshape(SEQ, D)))

def reference(hidden_in, cotangent, tile_depth, w_qkv, w_out, gain):
    start = (w_qkv, w_out, gain, jnp.zeros((3, D, INNER), jnp.float32), jnp.zeros((INNER, D), jnp.float32))
    carry, outs = lax.scan(doc_pass, start, (hidden_in, cotangent, tile_depth))
    return (outs[0], outs[1], carry[3], carry[4])
```

```python
import jax
import jax.numpy as jnp
from jax import lax
from jax.sharding import Mesh, PartitionSpec as P

HD = 128
TILE = 128
D = 2048
CTX = 8
NZ = 16
NY = 4
CHUNK = TILE // CTX
SCALE = HD**-0.5
CONTEXT = ("x", "core")
BF = jnp.bfloat16
F32 = jnp.float32


def swap(x, axis):
    return lax.all_to_all(x, axis, 0, 0)


def spread(x, axis, size):
    return swap(jnp.broadcast_to(x[None], (size,) + x.shape), axis)


def dot(a, b, dims):
    return lax.dot_general(a, b, (dims, ((), ())), preferred_element_type=F32)


def gather_weights(w_qkv, w_out):
    shard = jnp.concatenate([w_qkv, w_out.T[None]], 0)
    part = spread(shard, "z", NZ)
    full = spread(part, "y", NY)
    return full.transpose(2, 1, 0, 3, 4).reshape(4, D, HD)


def norm_chunk(x32, gain):
    inv = lax.rsqrt(jnp.mean(x32 * x32, -1, keepdims=True) + 1e-06)
    return inv, (x32 * inv * gain).astype(BF)


def all_rows(chunk):
    return spread(chunk, CONTEXT, CTX).reshape(TILE, D)


def sum_chunk(terms):
    return jnp.sum(swap(terms.astype(BF).reshape(CTX, CHUNK, D), CONTEXT).astype(F32), 0)


def forward(rows, w):
    q = dot(rows, w[0], ((1,), (0,))).astype(BF)
    k = dot(rows, w[1], ((1,), (0,))).astype(BF)
    v = dot(rows, w[2], ((1,), (0,))).astype(BF)
    pos = jnp.arange(TILE)
    scores = dot(q, k, ((1,), (1,))) * SCALE
    scores = jnp.where(pos[None, :] <= pos[:, None], scores, -1e30)
    expo = jnp.exp(scores - jnp.max(scores, -1, keepdims=True))
    prob = expo / jnp.sum(expo, -1, keepdims=True)
    probb = prob.astype(BF)
    attn = dot(probb, v, ((1,), (0,))).astype(BF)
    mixed = dot(attn, w[3], ((1,), (1,)))
    return mixed, (rows, q, k, v, prob, probb, attn)


def backward(dy, keep, w):
    rows, q, k, v, prob, probb, attn = keep
    dattn = dot(dy, w[3], ((1,), (0,))).astype(BF)
    delta = jnp.sum(dattn.astype(F32) * attn.astype(F32), -1, keepdims=True)
    dprob = dot(dattn, v, ((1,), (1,)))
    dscore = (prob * (dprob - delta) * SCALE).astype(BF)
    dq = dot(dscore, k, ((1,), (0,))).astype(BF)
    dk = dot(dscore, q, ((0,), (0,))).astype(BF)
    dv = dot(probb, dattn, ((0,), (0,))).astype(BF)
    dnorm = dot(dq, w[0], ((1,), (1,))) + dot(dk, w[1], ((1,), (1,))) + dot(dv, w[2], ((1,), (1,)))
    return dnorm, (dq, dk, dv)


def norm_grad(e, x32, inv, gain):
    u = e * gain
    return inv * u - x32 * inv**3 * jnp.mean(x32 * u, -1, keepdims=True)


def on_device(hidden_in, cotangent, tile_depth, w_qkv, w_out, gain):
    me = lax.axis_index("x") * 2 + lax.axis_index("core")
    depth = tile_depth[0]
    places = jnp.arange(CTX, dtype=jnp.int32)
    alive = depth >= 2
    owner = jnp.sum(jnp.where(alive, places, 0))
    live2 = jnp.any(alive)
    live3 = jnp.any(depth >= 3)
    mine = jnp.any(alive & (places == me))

    w = gather_weights(w_qkv, w_out)

    def owner_chunk(tile):
        got = swap(tile.reshape(CTX, CHUNK, D), CONTEXT)
        got = lax.dynamic_index_in_dim(got, owner, 0, keepdims=False)
        return jnp.where(live2, got, jnp.zeros_like(got))

    h1 = owner_chunk(hidden_in[0])
    g3 = owner_chunk(cotangent[0])

    x1 = h1.astype(F32)
    inv2, normed2 = norm_chunk(x1, gain)
    rows2 = all_rows(normed2)
    dy3 = all_rows(jnp.where(live3, g3, jnp.zeros_like(g3)))
    mixed2, keep2 = forward(rows2, w)
    h2 = (x1 + sum_chunk(mixed2)).astype(BF)

    x2 = h2.astype(F32)
    inv3, normed3 = norm_chunk(x2, gain)
    rows3 = all_rows(jnp.where(live3, normed3, jnp.zeros_like(normed3)))
    mixed3, keep3 = forward(rows3, w)
    dnorm3, (dq3, dk3, dv3) = backward(dy3, keep3, w)
    g2 = (g3.astype(F32) + norm_grad(sum_chunk(dnorm3), x2, inv3, gain)).astype(BF)
    h3 = (x2 + sum_chunk(mixed3)).astype(BF)

    dy2 = all_rows(g2)
    dnorm2, (dq2, dk2, dv2) = backward(dy2, keep2, w)
    g1 = (g2.astype(F32) + norm_grad(sum_chunk(dnorm2), x1, inv2, gain)).astype(BF)

    def weight_grad(left3, right3, left2, right2):
        left = jnp.concatenate([left3, left2], 0)
        right = jnp.concatenate([right3, right2], 0)
        return dot(left, right, ((0,), (0,))).astype(BF)

    grads = jnp.stack(
        [
            weight_grad(rows3, dq3, rows2, dq2),
            weight_grad(rows3, dk3, rows2, dk2),
            weight_grad(rows3, dv3, rows2, dv2),
            weight_grad(dy3, keep3[-1], dy2, keep2[-1]),
        ]
    )
    grads = grads.reshape(4, NZ, NY, 32, HD).transpose(2, 1, 0, 3, 4)
    part = jnp.sum(swap(grads, "y").astype(F32), 0).astype(BF)
    shard = jnp.sum(swap(part, "z").astype(F32), 0)

    back_h = all_rows(h3)
    back_g = all_rows(g1)
    hidden_out = jnp.where(mine, back_h, hidden_in[0])
    grad_in = jnp.where(mine, back_g, cotangent[0])
    return (hidden_out[None], grad_in[None], shard[:3], shard[3].T)


def solution(mesh):
    grid = Mesh(mesh.devices.reshape(NZ, NY, CTX // 2, 2), ("z", "y") + CONTEXT)
    dp = ("z", "y")
    in_specs = (
        P(dp, CONTEXT, None),
        P(dp, CONTEXT, None),
        P(dp, None),
        P(None, dp, CONTEXT),
        P(CONTEXT, dp),
        P(),
    )
    out_specs = (
        P(dp, CONTEXT, None),
        P(dp, CONTEXT, None),
        P(None, dp, CONTEXT),
        P(CONTEXT, dp),
    )
    return jax.shard_map(
        on_device, mesh=grid, in_specs=in_specs, out_specs=out_specs, check_vma=False
    )
```

```python
import jax
import jax.numpy as jnp
from jax import lax
from jax.sharding import Mesh, PartitionSpec as P

HD = 128
TILE = 128
D = 2048
CTX = 8
NZ = 16
NY = 4
CHUNK = TILE // CTX
SCALE = HD**-0.5
CONTEXT = ("x", "core")
BF = jnp.bfloat16
F32 = jnp.float32


def swap(x, axis):
    return lax.all_to_all(x, axis, 0, 0)


def spread(x, axis, size):
    return swap(jnp.broadcast_to(x[None], (size,) + x.shape), axis)


def dot(a, b, dims):
    return lax.dot_general(a, b, (dims, ((), ())), preferred_element_type=F32)


def add(a, b):
    return (a.astype(F32) + b.astype(F32)).astype(BF)


def from_core(x):
    return lax.ppermute(x, "core", [(0, 1), (1, 0)])


def from_pair(x, bit):
    return lax.ppermute(x, "x", [(i, i ^ bit) for i in range(CTX // 2)])


def y_pieces(part):
    y = lax.axis_index("y")
    part = part.transpose(1, 0, 2, 3)[:, :, None]
    full = jnp.zeros((part.shape[0], NZ, NY, 32, HD), BF)
    full = lax.dynamic_update_index_in_dim(full, part, y, 2)
    for k in range(1, NY):
        got = lax.ppermute(part, "y", [(i, (i + k) % NY) for i in range(NY)])
        full = lax.dynamic_update_index_in_dim(full, got, (y - k) % NY, 2)
    return full.reshape(-1, D, HD)


def gather_weights(w_qkv, w_out):
    first = spread(w_qkv[:2], "z", NZ)
    second = spread(jnp.stack([w_qkv[2], w_out.T]), "z", NZ)
    wa, wb = y_pieces(first), y_pieces(second)
    return wa[0], wa[1], wb[0], wb[1]


def from_owner(tile, mine):
    kept = jnp.where(mine, tile, jnp.zeros_like(tile))
    kept = kept + from_core(kept)
    kept = kept + from_pair(kept, 1)
    return kept + from_pair(kept, 3)


def sum_tile(terms):
    core = lax.axis_index("core")
    halves = terms.astype(BF).reshape(2, TILE // 2, D)
    part = lax.dynamic_index_in_dim(halves, core, 0, keepdims=False)
    part = add(part, from_core(lax.dynamic_index_in_dim(halves, 1 - core, 0, keepdims=False)))
    part = add(part, from_pair(part, 1))
    part = add(part, from_pair(part, 3))
    other = from_core(part)
    low, high = jnp.where(core == 0, part, other), jnp.where(core == 0, other, part)
    return jnp.concatenate([low, high], 0).astype(F32)


def norm_chunk(x32, gain):
    inv = lax.rsqrt(jnp.mean(x32 * x32, -1, keepdims=True) + 1e-06)
    return inv, (x32 * inv * gain).astype(BF)


def all_rows(chunk):
    return lax.all_gather(chunk, CONTEXT, tiled=True)


def sum_chunk(terms):
    return jnp.sum(swap(terms.astype(BF).reshape(CTX, CHUNK, D), CONTEXT).astype(F32), 0)


def forward(rows, w):
    q = dot(rows, w[0], ((1,), (0,))).astype(BF)
    k = dot(rows, w[1], ((1,), (0,))).astype(BF)
    v = dot(rows, w[2], ((1,), (0,))).astype(BF)
    pos = jnp.arange(TILE)
    scores = dot(q, k, ((1,), (1,))) * SCALE
    scores = jnp.where(pos[None, :] <= pos[:, None], scores, -1e30)
    expo = jnp.exp(scores - jnp.max(scores, -1, keepdims=True))
    prob = expo / jnp.sum(expo, -1, keepdims=True)
    probb = prob.astype(BF)
    attn = dot(probb, v, ((1,), (0,))).astype(BF)
    mixed = dot(attn, w[3], ((1,), (1,)))
    return mixed, (rows, q, k, v, prob, probb, attn)


def backward(dy, keep, w):
    rows, q, k, v, prob, probb, attn = keep
    dattn = dot(dy, w[3], ((1,), (0,))).astype(BF)
    delta = jnp.sum(dattn.astype(F32) * attn.astype(F32), -1, keepdims=True)
    dprob = dot(dattn, v, ((1,), (1,)))
    dscore = (prob * (dprob - delta) * SCALE).astype(BF)
    dq = dot(dscore, k, ((1,), (0,))).astype(BF)
    dk = dot(dscore, q, ((0,), (0,))).astype(BF)
    dv = dot(probb, dattn, ((0,), (0,))).astype(BF)
    dnorm = dot(dq, w[0], ((1,), (1,))) + dot(dk, w[1], ((1,), (1,))) + dot(dv, w[2], ((1,), (1,)))
    return dnorm, (dq, dk, dv)


def norm_grad(e, x32, inv, gain):
    u = e * gain
    return inv * u - x32 * inv**3 * jnp.mean(x32 * u, -1, keepdims=True)


def on_device(hidden_in, cotangent, tile_depth, w_qkv, w_out, gain):
    me = lax.axis_index("x") * 2 + lax.axis_index("core")
    depth = tile_depth[0]
    places = jnp.arange(CTX, dtype=jnp.int32)
    alive = depth >= 2
    live3 = jnp.any(depth >= 3)
    mine = jnp.any(alive & (places == me))

    w = gather_weights(w_qkv, w_out)

    def chunk(tile):
        return lax.dynamic_index_in_dim(tile.reshape(CTX, CHUNK, D), me, 0, keepdims=False)

    h1 = from_owner(hidden_in[0], mine)
    g3 = from_owner(cotangent[0], mine)
    dy3 = jnp.where(live3, g3, jnp.zeros_like(g3))

    x1 = h1.astype(F32)
    inv2, rows2 = norm_chunk(x1, gain)
    mixed2, keep2 = forward(rows2, w)
    h2 = all_rows((chunk(h1).astype(F32) + sum_chunk(mixed2)).astype(BF))

    x2 = h2.astype(F32)
    inv3, normed3 = norm_chunk(x2, gain)
    rows3 = jnp.where(live3, normed3, jnp.zeros_like(normed3))
    mixed3, keep3 = forward(rows3, w)
    dnorm3, (dq3, dk3, dv3) = backward(dy3, keep3, w)
    x2c = chunk(h2).astype(F32)
    inv3c, _ = norm_chunk(x2c, gain)
    g2c = chunk(g3).astype(F32) + norm_grad(sum_chunk(dnorm3), x2c, inv3c, gain)
    g2 = all_rows(g2c.astype(BF))

    dy2 = g2
    dnorm2, (dq2, dk2, dv2) = backward(dy2, keep2, w)

    def weight_grad(left3, right3, left2, right2):
        left = jnp.concatenate([left3, left2], 0)
        right = jnp.concatenate([right3, right2], 0)
        return dot(left, right, ((0,), (0,))).astype(BF)

    grads = jnp.stack(
        [
            weight_grad(rows3, dq3, rows2, dq2),
            weight_grad(rows3, dk3, rows2, dk2),
            weight_grad(rows3, dv3, rows2, dv2),
            weight_grad(dy3, keep3[-1], dy2, keep2[-1]),
        ]
    )
    grads = grads.reshape(4, NZ, NY, 32, HD).transpose(2, 1, 0, 3, 4)
    part = jnp.sum(swap(grads, "y").astype(F32), 0).astype(BF)
    shard = jnp.sum(swap(part, "z").astype(F32), 0)

    h3 = (x2 + sum_tile(mixed3)).astype(BF)
    g1 = (g2.astype(F32) + norm_grad(sum_tile(dnorm2), x1, inv2, gain)).astype(BF)
    hidden_out = jnp.where(mine, h3, hidden_in[0])
    grad_in = jnp.where(mine, g1, cotangent[0])
    return (hidden_out[None], grad_in[None], shard[:3], shard[3].T)


def solution(mesh):
    grid = Mesh(mesh.devices.reshape(NZ, NY, CTX // 2, 2), ("z", "y") + CONTEXT)
    dp = ("z", "y")
    in_specs = (
        P(dp, CONTEXT, None),
        P(dp, CONTEXT, None),
        P(dp, None),
        P(None, dp, CONTEXT),
        P(CONTEXT, dp),
        P(),
    )
    out_specs = (
        P(dp, CONTEXT, None),
        P(dp, CONTEXT, None),
        P(None, dp, CONTEXT),
        P(CONTEXT, dp),
    )
    return jax.shard_map(
        on_device, mesh=grid, in_specs=in_specs, out_specs=out_specs, check_vma=False
    )
```

```python
import jax
import jax.numpy as jnp
from jax import lax
from jax.sharding import Mesh, PartitionSpec as P

HD = 128
TILE = 128
D = 2048
CTX = 8
NZ = 16
NY = 4
CHUNK = TILE // CTX
SCALE = HD**-0.5
CONTEXT = ("x", "core")
BF = jnp.bfloat16
F32 = jnp.float32


def swap(x, axis):
    return lax.all_to_all(x, axis, 0, 0)


def spread(x, axis, size):
    return swap(jnp.broadcast_to(x[None], (size,) + x.shape), axis)


def dot(a, b, dims):
    return lax.dot_general(a, b, (dims, ((), ())), preferred_element_type=F32)


def add(a, b):
    return (a.astype(F32) + b.astype(F32)).astype(BF)


def from_core(x):
    return lax.ppermute(x, "core", [(0, 1), (1, 0)])


def from_pair(x, bit):
    return lax.ppermute(x, "x", [(i, i ^ bit) for i in range(CTX // 2)])


def from_zpair(x):
    return lax.ppermute(x, "zq", [(0, 1), (1, 0)])


def y_others(pieces):
    y = lax.axis_index("y")
    out = []
    for k in range(1, NY):
        got = lax.ppermute(pieces(k), "y", [(i, (i + k) % NY) for i in range(NY)])
        out.append(((y - k) % NY, got))
    return out


def gather_weights(w_qkv, w_out):
    y, zq = lax.axis_index("y"), lax.axis_index("zq")
    shard = jnp.concatenate([w_qkv, w_out.T[None]], 0)
    near = spread(shard, "zp", NZ // 2)
    full = jnp.zeros((4, NZ // 2, 2, NY, 32, HD), BF)
    for parity, part in ((zq, near), (1 - zq, from_zpair(near))):
        for source, piece in [(y, part)] + y_others(lambda k: part):
            piece = piece.transpose(1, 0, 2, 3)[:, :, None, None]
            full = lax.dynamic_update_slice(full, piece, (0, 0, parity, source, 0, 0))
    return full.reshape(4, D, HD)


def by_feature(x):
    return x.reshape(NZ, NY, 32, x.shape[-1])


def for_y(blocks, k):
    return lax.dynamic_index_in_dim(blocks, (lax.axis_index("y") + k) % NY, 1, keepdims=False)


def scatter_z(quarter):
    zq = lax.axis_index("zq")
    pairs = quarter.reshape(NZ // 2, 2, 4, 32, HD)
    mine = lax.dynamic_index_in_dim(pairs, zq, 1, keepdims=False)
    other = lax.dynamic_index_in_dim(pairs, 1 - zq, 1, keepdims=False)
    part = mine + from_zpair(other.astype(BF)).astype(F32)
    return jnp.sum(swap(part.astype(BF), "zp").astype(F32), 0)


def from_owner(tile, mine):
    kept = jnp.where(mine, tile, jnp.zeros_like(tile))
    kept = kept + from_core(kept)
    kept = kept + from_pair(kept, 1)
    return kept + from_pair(kept, 3)


def sum_begin(terms):
    core = lax.axis_index("core")
    halves = terms.astype(BF).reshape(2, TILE // 2, D)
    part = lax.dynamic_index_in_dim(halves, core, 0, keepdims=False)
    part = add(part, from_core(lax.dynamic_index_in_dim(halves, 1 - core, 0, keepdims=False)))
    return add(part, from_pair(part, 1))


def sum_end(part):
    core = lax.axis_index("core")
    part = add(part, from_pair(part, 3))
    other = from_core(part)
    low, high = jnp.where(core == 0, part, other), jnp.where(core == 0, other, part)
    return jnp.concatenate([low, high], 0).astype(F32)


def norm_chunk(x32, gain):
    inv = lax.rsqrt(jnp.mean(x32 * x32, -1, keepdims=True) + 1e-06)
    return inv, (x32 * inv * gain).astype(BF)


def all_rows(chunk):
    return lax.all_gather(chunk, CONTEXT, tiled=True)


def sum_chunk(terms):
    return jnp.sum(swap(terms.astype(BF).reshape(CTX, CHUNK, D), CONTEXT).astype(F32), 0)


def forward(rows, w):
    q = dot(rows, w[0], ((1,), (0,))).astype(BF)
    k = dot(rows, w[1], ((1,), (0,))).astype(BF)
    v = dot(rows, w[2], ((1,), (0,))).astype(BF)
    pos = jnp.arange(TILE)
    scores = dot(q, k, ((1,), (1,))) * SCALE
    scores = jnp.where(pos[None, :] <= pos[:, None], scores, -1e30)
    expo = jnp.exp(scores - jnp.max(scores, -1, keepdims=True))
    prob = expo / jnp.sum(expo, -1, keepdims=True)
    probb = prob.astype(BF)
    attn = dot(probb, v, ((1,), (0,))).astype(BF)
    mixed = dot(attn, w[3], ((1,), (1,)))
    return mixed, (rows, q, k, v, prob, probb, attn)


def backward(dy, keep, w):
    rows, q, k, v, prob, probb, attn = keep
    dattn = dot(dy, w[3], ((1,), (0,))).astype(BF)
    delta = jnp.sum(dattn.astype(F32) * attn.astype(F32), -1, keepdims=True)
    dprob = dot(dattn, v, ((1,), (1,)))
    dscore = (prob * (dprob - delta) * SCALE).astype(BF)
    dq = dot(dscore, k, ((1,), (0,))).astype(BF)
    dk = dot(dscore, q, ((0,), (0,))).astype(BF)
    dv = dot(probb, dattn, ((0,), (0,))).astype(BF)
    dnorm = dot(dq, w[0], ((1,), (1,))) + dot(dk, w[1], ((1,), (1,))) + dot(dv, w[2], ((1,), (1,)))
    return dnorm, (dq, dk, dv)


def norm_grad(e, x32, inv, gain):
    u = e * gain
    return inv * u - x32 * inv**3 * jnp.mean(x32 * u, -1, keepdims=True)


def on_device(hidden_in, cotangent, tile_depth, w_qkv, w_out, gain):
    me = lax.axis_index("x") * 2 + lax.axis_index("core")
    depth = tile_depth[0]
    places = jnp.arange(CTX, dtype=jnp.int32)
    alive = depth >= 2
    live3 = jnp.any(depth >= 3)
    mine = jnp.any(alive & (places == me))

    w = gather_weights(w_qkv, w_out)

    def chunk(tile):
        return lax.dynamic_index_in_dim(tile.reshape(CTX, CHUNK, D), me, 0, keepdims=False)

    tokens = ((0,), (0,))
    h1 = from_owner(hidden_in[0], mine)
    g3 = from_owner(cotangent[0], mine)

    x1 = h1.astype(F32)
    inv2, rows2 = norm_chunk(x1, gain)
    mixed2, keep2 = forward(rows2, w)
    attn2 = keep2[-1]
    rows2t = by_feature(rows2.T)
    rows_in = y_others(lambda k: for_y(rows2t, k))
    h2 = all_rows((chunk(h1).astype(F32) + sum_chunk(mixed2)).astype(BF))
    h2, rows_in = lax.optimization_barrier((h2, rows_in))

    x2 = h2.astype(F32)
    inv3, normed3 = norm_chunk(x2, gain)
    rows3 = jnp.where(live3, normed3, jnp.zeros_like(normed3))
    dy3 = jnp.where(live3, g3, jnp.zeros_like(g3))
    mixed3, keep3 = forward(rows3, w)
    h3_part = sum_begin(mixed3)
    dnorm3, (dq3, dk3, dv3) = backward(dy3, keep3, w)
    dnorm3, dq3, dk3, dv3 = lax.optimization_barrier((dnorm3.astype(BF), dq3, dk3, dv3))
    early = jnp.stack(
        [by_feature(dot(rows3, d, tokens)) for d in (dq3, dk3, dv3)]
        + [by_feature(dot(dy3, keep3[-1], tokens))],
        2,
    )
    early_in = y_others(lambda k: for_y(early, k).astype(BF))
    x2c = chunk(h2).astype(F32)
    inv3c, _ = norm_chunk(x2c, gain)
    g2c = chunk(g3).astype(F32) + norm_grad(sum_chunk(dnorm3), x2c, inv3c, gain)
    g2 = spread(g2c.astype(BF), CONTEXT, CTX).reshape(TILE, D)
    g2, h3_part = lax.optimization_barrier((g2, h3_part))

    dnorm2, (dq2, dk2, dv2) = backward(g2, keep2, w)
    dnorm2 = dnorm2.astype(BF)
    g1_part = sum_begin(dnorm2)
    out2 = dot(g2, attn2, tokens)
    dqkv2 = jnp.broadcast_to(jnp.concatenate([dq2, dk2, dv2], 0)[None], (NY, 3 * TILE, HD))
    out2y = by_feature(out2).transpose(1, 0, 2, 3).reshape(NY, D // NY, HD).astype(BF)
    late, early_in = lax.optimization_barrier((jnp.concatenate([dqkv2, out2y], 1), early_in))
    late = swap(late, "y")

    y = lax.axis_index("y")
    left = jnp.zeros((D // NY, NY, TILE), BF)
    for source, piece in [(y, for_y(rows2t, 0))] + rows_in:
        left = lax.dynamic_update_slice(left, piece.reshape(D // NY, 1, TILE), (0, source, 0))
    right = late[:, : 3 * TILE].reshape(NY, 3, TILE, HD)
    quarter = jnp.einsum("dyr,ytrc->dtc", left, right, preferred_element_type=F32)
    quarter = quarter.reshape(NZ, 32, 3, HD).transpose(0, 2, 1, 3)
    last = jnp.sum(late[:, 3 * TILE :].astype(F32), 0).reshape(NZ, 1, 32, HD)
    quarter = jnp.concatenate([quarter, last], 1)
    quarter = quarter + for_y(early, 0) + sum(x.astype(F32) for _, x in early_in)
    shard = scatter_z(quarter)

    h3 = (x2 + sum_end(h3_part)).astype(BF)
    g1 = (g2.astype(F32) + norm_grad(sum_end(g1_part), x1, inv2, gain)).astype(BF)
    hidden_out = jnp.where(mine, h3, hidden_in[0])
    grad_in = jnp.where(mine, g1, cotangent[0])
    return (hidden_out[None], grad_in[None], shard[:3], shard[3].T)


def solution(mesh):
    grid = Mesh(mesh.devices.reshape(NZ // 2, 2, NY, CTX // 2, 2), ("zp", "zq", "y") + CONTEXT)
    dp = ("zp", "zq", "y")
    in_specs = (
        P(dp, CONTEXT, None),
        P(dp, CONTEXT, None),
        P(dp, None),
        P(None, dp, CONTEXT),
        P(CONTEXT, dp),
        P(),
    )
    out_specs = (
        P(dp, CONTEXT, None),
        P(dp, CONTEXT, None),
        P(None, dp, CONTEXT),
        P(CONTEXT, dp),
    )
    return jax.shard_map(
        on_device, mesh=grid, in_specs=in_specs, out_specs=out_specs, check_vma=False
    )
```

```python
import jax
import jax.numpy as jnp
from jax import lax
from jax.sharding import Mesh, PartitionSpec as P

HD = 128
TILE = 128
D = 2048
CTX = 8
NP = 8
NN = 8
NEAR = ("zq", "y")
CHUNK = TILE // CTX
SCALE = HD**-0.5
CONTEXT = ("x", "core")
BF = jnp.bfloat16
F32 = jnp.float32


def swap(x, axis):
    return lax.all_to_all(x, axis, 0, 0)


def spread(x, axis, size):
    return swap(jnp.broadcast_to(x[None], (size,) + x.shape), axis)


def dot(a, b, dims):
    return lax.dot_general(a, b, (dims, ((), ())), preferred_element_type=F32)


def add(a, b):
    return (a.astype(F32) + b.astype(F32)).astype(BF)


def from_core(x):
    return lax.ppermute(x, "core", [(0, 1), (1, 0)])


def from_pair(x, bit):
    return lax.ppermute(x, "x", [(i, i ^ bit) for i in range(CTX // 2)])


def for_near(x):
    return x.reshape(NP, NN, 32, x.shape[-1]).transpose(1, 0, 2, 3).reshape(NN, D // NN, -1)


def sum_begin(terms):
    core = lax.axis_index("core")
    halves = terms.astype(BF).reshape(2, TILE // 2, D)
    part = lax.dynamic_index_in_dim(halves, core, 0, keepdims=False)
    part = add(part, from_core(lax.dynamic_index_in_dim(halves, 1 - core, 0, keepdims=False)))
    return add(part, from_pair(part, 1))


def sum_end(parts):
    core = lax.axis_index("core")
    part = jnp.stack(parts)
    part = add(part, from_pair(part, 3))
    other = from_core(part)
    low, high = jnp.where(core == 0, part, other), jnp.where(core == 0, other, part)
    whole = jnp.concatenate([low, high], 1).astype(F32)
    return whole[0], whole[1]


def norm_chunk(x32, gain):
    inv = lax.rsqrt(jnp.mean(x32 * x32, -1, keepdims=True) + 1e-06)
    return inv, (x32 * inv * gain).astype(BF)


def all_rows(chunk):
    return lax.all_gather(chunk, CONTEXT, tiled=True)


def sum_chunk(terms):
    return jnp.sum(swap(terms.astype(BF).reshape(CTX, CHUNK, D), CONTEXT).astype(F32), 0)


def forward(rows, w):
    q = dot(rows, w[0], ((1,), (0,))).astype(BF)
    k = dot(rows, w[1], ((1,), (0,))).astype(BF)
    v = dot(rows, w[2], ((1,), (0,))).astype(BF)
    pos = jnp.arange(TILE)
    scores = dot(q, k, ((1,), (1,))) * SCALE
    scores = jnp.where(pos[None, :] <= pos[:, None], scores, -1e30)
    expo = jnp.exp(scores - jnp.max(scores, -1, keepdims=True))
    prob = expo / jnp.sum(expo, -1, keepdims=True)
    probb = prob.astype(BF)
    attn = dot(probb, v, ((1,), (0,))).astype(BF)
    mixed = dot(attn, w[3], ((1,), (1,)))
    return mixed, (rows, q, k, v, prob, probb, attn)


def backward(dy, keep, w):
    rows, q, k, v, prob, probb, attn = keep
    dattn = dot(dy, w[3], ((1,), (0,))).astype(BF)
    delta = jnp.sum(dattn.astype(F32) * attn.astype(F32), -1, keepdims=True)
    dprob = dot(dattn, v, ((1,), (1,)))
    dscore = (prob * (dprob - delta) * SCALE).astype(BF)
    dq = dot(dscore, k, ((1,), (0,))).astype(BF)
    dk = dot(dscore, q, ((0,), (0,))).astype(BF)
    dv = dot(probb, dattn, ((0,), (0,))).astype(BF)
    dnorm = dot(dq, w[0], ((1,), (1,))) + dot(dk, w[1], ((1,), (1,))) + dot(dv, w[2], ((1,), (1,)))
    return dnorm, (dq, dk, dv)


def norm_grad(e, x32, inv, gain):
    u = e * gain
    return inv * u - x32 * inv**3 * jnp.mean(x32 * u, -1, keepdims=True)


def on_device(hidden_in, cotangent, tile_depth, w_qkv, w_out, gain):
    me = lax.axis_index("x") * 2 + lax.axis_index("core")
    depth = tile_depth[0]
    places = jnp.arange(CTX, dtype=jnp.int32)
    alive = depth >= 2
    live3 = jnp.any(depth >= 3)
    mine = jnp.any(alive & (places == me))

    def chunk(tile):
        return lax.dynamic_index_in_dim(tile.reshape(CTX, CHUNK, D), me, 0, keepdims=False)

    tokens = ((0,), (0,))
    core = lax.axis_index("core")
    none = jnp.zeros_like(hidden_in[0])
    h_part = jnp.where(mine, hidden_in[0], none)
    g_part = jnp.where(mine, cotangent[0], none)
    tile = jnp.where(core == 0, h_part, g_part) + from_core(jnp.where(core == 0, g_part, h_part))
    tile = tile + from_pair(tile, 1)

    near = spread(jnp.concatenate([w_qkv, w_out.T[None]], 0), "zp", NP)
    near, tile = lax.optimization_barrier((near, tile))
    w = spread(near, NEAR, NN).transpose(2, 1, 0, 3, 4).reshape(4, D, HD)
    tile = tile + from_pair(tile, 3)
    other = from_core(tile)
    h1, g3 = jnp.where(core == 0, tile, other), jnp.where(core == 0, other, tile)

    x1 = h1.astype(F32)
    inv2, rows2 = norm_chunk(x1, gain)
    mixed2, keep2 = forward(rows2, w)
    attn2 = keep2[-1]
    h2c = (chunk(h1).astype(F32) + sum_chunk(mixed2)).astype(BF)
    h2c, rows2t = lax.optimization_barrier((h2c, for_near(rows2.T)))
    rows_in = swap(rows2t, NEAR)
    h2 = all_rows(h2c)
    h2, rows_in = lax.optimization_barrier((h2, rows_in))

    x2 = h2.astype(F32)
    inv3, normed3 = norm_chunk(x2, gain)
    rows3 = jnp.where(live3, normed3, jnp.zeros_like(normed3))
    dy3 = jnp.where(live3, g3, jnp.zeros_like(g3))
    mixed3, keep3 = forward(rows3, w)
    dnorm3, (dq3, dk3, dv3) = backward(dy3, keep3, w)
    dnorm3, dq3, dk3, dv3 = lax.optimization_barrier((dnorm3.astype(BF), dq3, dk3, dv3))
    h3_part = sum_begin(mixed3)
    early = jnp.concatenate(
        [for_near(dot(rows3, d, tokens).astype(BF)) for d in (dq3, dk3, dv3)]
        + [for_near(dot(dy3, keep3[-1], tokens).astype(BF))],
        -1,
    )
    x2c = chunk(h2).astype(F32)
    inv3c, _ = norm_chunk(x2c, gain)
    g2c = chunk(g3).astype(F32) + norm_grad(sum_chunk(dnorm3), x2c, inv3c, gain)
    g2c, early = lax.optimization_barrier((g2c.astype(BF), early))
    early_in = swap(early, NEAR)
    g2 = all_rows(g2c)
    g2, h3_part = lax.optimization_barrier((g2, h3_part))

    dnorm2, (dq2, dk2, dv2) = backward(g2, keep2, w)
    dnorm2 = dnorm2.astype(BF)
    out2 = for_near(dot(g2, attn2, tokens).astype(BF))
    dqkv2 = jnp.broadcast_to(jnp.concatenate([dq2, dk2, dv2], 0)[None], (NN, 3 * TILE, HD))
    late = jnp.concatenate([dqkv2, out2], 1)
    late, early_in = lax.optimization_barrier((late, early_in))
    late = swap(late, NEAR)

    right = late[:, : 3 * TILE].reshape(NN, 3, TILE, HD)
    part = jnp.einsum("ndr,ntrc->dtc", rows_in, right, preferred_element_type=F32)
    last = jnp.sum(late[:, 3 * TILE :].astype(F32), 0)
    part = jnp.concatenate([part.reshape(D // NN, 3 * HD), last], 1)
    part = (part + jnp.sum(early_in.astype(F32), 0)).astype(BF)
    part = part.reshape(NP, 32, 4, HD).transpose(0, 2, 1, 3)
    shard = jnp.sum(swap(part, "zp").astype(F32), 0)

    sum3, sum2 = sum_end([h3_part, sum_begin(dnorm2)])
    h3 = (x2 + sum3).astype(BF)
    g1 = (g2.astype(F32) + norm_grad(sum2, x1, inv2, gain)).astype(BF)
    hidden_out = jnp.where(mine, h3, hidden_in[0])
    grad_in = jnp.where(mine, g1, cotangent[0])
    return (hidden_out[None], grad_in[None], shard[:3], shard[3].T)


def solution(mesh):
    grid = Mesh(mesh.devices.reshape(NP, 2, NN // 2, CTX // 2, 2), ("zp", "zq", "y") + CONTEXT)
    dp = ("zp", "zq", "y")
    in_specs = (
        P(dp, CONTEXT, None),
        P(dp, CONTEXT, None),
        P(dp, None),
        P(None, dp, CONTEXT),
        P(CONTEXT, dp),
        P(),
    )
    out_specs = (
        P(dp, CONTEXT, None),
        P(dp, CONTEXT, None),
        P(None, dp, CONTEXT),
        P(CONTEXT, dp),
    )
    return jax.shard_map(
        on_device, mesh=grid, in_specs=in_specs, out_specs=out_specs, check_vma=False
    )
```

```python
import jax
import jax.numpy as jnp
from jax import lax
from jax.sharding import Mesh, PartitionSpec as P

HD = 128
TILE = 128
D = 2048
CTX = 8
NP = 8
NN = 8
NEAR = ("zq", "y")
CHUNK = TILE // CTX
SCALE = HD**-0.5
CONTEXT = ("x", "core")
BF = jnp.bfloat16
F32 = jnp.float32


def swap(x, axis):
    return lax.all_to_all(x, axis, 0, 0)


def spread(x, axis, size):
    return swap(jnp.broadcast_to(x[None], (size,) + x.shape), axis)


def dot(a, b, dims):
    return lax.dot_general(a, b, (dims, ((), ())), preferred_element_type=F32)


def add(a, b):
    return (a.astype(F32) + b.astype(F32)).astype(BF)


def from_core(x):
    return lax.ppermute(x, "core", [(0, 1), (1, 0)])


def from_pair(x, bit):
    return lax.ppermute(x, "x", [(i, i ^ bit) for i in range(CTX // 2)])


def norm_chunk(x32, gain):
    inv = lax.rsqrt(jnp.mean(x32 * x32, -1, keepdims=True) + 1e-06)
    return inv, (x32 * inv * gain).astype(BF)


def all_rows(chunk):
    return lax.all_gather(chunk, CONTEXT, tiled=True)


def sum_chunk(terms):
    return jnp.sum(swap(terms.astype(BF).reshape(CTX, CHUNK, D), CONTEXT).astype(F32), 0)


def forward(rows, w):
    q = dot(rows, w[0], ((1,), (0,))).astype(BF)
    k = dot(rows, w[1], ((1,), (0,))).astype(BF)
    v = dot(rows, w[2], ((1,), (0,))).astype(BF)
    pos = jnp.arange(TILE)
    scores = dot(q, k, ((1,), (1,))) * SCALE
    scores = jnp.where(pos[None, :] <= pos[:, None], scores, -1e30)
    expo = jnp.exp(scores - jnp.max(scores, -1, keepdims=True))
    prob = expo / jnp.sum(expo, -1, keepdims=True)
    probb = prob.astype(BF)
    attn = dot(probb, v, ((1,), (0,))).astype(BF)
    mixed = dot(attn, w[3], ((1,), (1,)))
    return mixed, (rows, q, k, v, prob, probb, attn)


def backward(dy, keep, w):
    rows, q, k, v, prob, probb, attn = keep
    dattn = dot(dy, w[3], ((1,), (0,))).astype(BF)
    delta = jnp.sum(dattn.astype(F32) * attn.astype(F32), -1, keepdims=True)
    dprob = dot(dattn, v, ((1,), (1,)))
    dscore = (prob * (dprob - delta) * SCALE).astype(BF)
    dq = dot(dscore, k, ((1,), (0,))).astype(BF)
    dk = dot(dscore, q, ((0,), (0,))).astype(BF)
    dv = dot(probb, dattn, ((0,), (0,))).astype(BF)
    return dq, dk, dv


def norm_terms(dqkv, w):
    dq, dk, dv = dqkv
    total = dot(dq, w[0], ((1,), (1,))) + dot(dk, w[1], ((1,), (1,))) + dot(dv, w[2], ((1,), (1,)))
    return total.astype(BF)


def norm_grad(e, x32, inv, gain):
    u = e * gain
    return inv * u - x32 * inv**3 * jnp.mean(x32 * u, -1, keepdims=True)


def on_device(hidden_in, cotangent, tile_depth, w_qkv, w_out, gain):
    me = lax.axis_index("x") * 2 + lax.axis_index("core")
    depth = tile_depth[0]
    places = jnp.arange(CTX, dtype=jnp.int32)
    alive = depth >= 2
    live3 = jnp.any(depth >= 3)
    mine = jnp.any(alive & (places == me))

    def chunk(tile):
        return lax.dynamic_index_in_dim(tile.reshape(CTX, CHUNK, D), me, 0, keepdims=False)

    tokens = ((0,), (0,))
    core = lax.axis_index("core")
    none = jnp.zeros_like(hidden_in[0])
    h_part = jnp.where(mine, hidden_in[0], none)
    g_part = jnp.where(mine, cotangent[0], none)
    tile = jnp.where(core == 0, h_part, g_part) + from_core(jnp.where(core == 0, g_part, h_part))
    tile = tile + from_pair(tile, 1)

    near = spread(jnp.concatenate([w_qkv, w_out.T[None]], 0), "zp", NP)
    near, tile = lax.optimization_barrier((near, tile))
    w = spread(near, NEAR, NN).transpose(2, 1, 0, 3, 4).reshape(4, D, HD)
    tile = tile + from_pair(tile, 3)
    other = from_core(tile)
    h1, g3 = jnp.where(core == 0, tile, other), jnp.where(core == 0, other, tile)

    x1 = h1.astype(F32)
    inv2, rows2 = norm_chunk(x1, gain)
    mixed2, keep2 = forward(rows2, w)
    attn2 = keep2[-1]
    h2c = (chunk(h1).astype(F32) + sum_chunk(mixed2)).astype(BF)
    h2 = all_rows(h2c)

    x2 = h2.astype(F32)
    inv3, normed3 = norm_chunk(x2, gain)
    rows3 = jnp.where(live3, normed3, jnp.zeros_like(normed3))
    dy3 = jnp.where(live3, g3, jnp.zeros_like(g3))
    mixed3, keep3 = forward(rows3, w)
    dqkv3 = backward(dy3, keep3, w)
    dnorm3, dqkv3 = lax.optimization_barrier((norm_terms(dqkv3, w), dqkv3))

    def products(rows, dqkv, dy, attn):
        terms = [dot(rows, d, tokens) for d in dqkv] + [dot(dy, attn, tokens)]
        return jnp.stack([x.reshape(NP, NN, 32, HD) for x in terms], 2)

    early = products(rows3, dqkv3, dy3, keep3[-1])
    x2c = chunk(h2).astype(F32)
    inv3c, _ = norm_chunk(x2c, gain)
    g2c = chunk(g3).astype(F32) + norm_grad(sum_chunk(dnorm3), x2c, inv3c, gain)
    g2c, early = lax.optimization_barrier((g2c.astype(BF), early))
    g2 = all_rows(g2c)

    dqkv2 = backward(g2, keep2, w)
    terms = (early + products(rows2, dqkv2, g2, attn2)).astype(BF).transpose(1, 0, 2, 3, 4)
    terms, dqkv2 = lax.optimization_barrier((terms, dqkv2))
    terms = swap(terms, NEAR)
    dnorm2 = norm_terms(dqkv2, w)

    mixed3 = mixed3.astype(BF)
    tile = add(jnp.where(core == 0, mixed3, dnorm2), from_core(jnp.where(core == 0, dnorm2, mixed3)))
    tile = add(tile, from_pair(tile, 1))
    terms, tile = lax.optimization_barrier((terms, tile))

    part = jnp.sum(terms.astype(F32), 0).astype(BF)
    shard = jnp.sum(swap(part, "zp").astype(F32), 0)

    tile = add(tile, from_pair(tile, 3))
    other = from_core(tile)
    sum3, sum2 = jnp.where(core == 0, tile, other), jnp.where(core == 0, other, tile)
    h3 = (x2 + sum3.astype(F32)).astype(BF)
    g1 = (g2.astype(F32) + norm_grad(sum2.astype(F32), x1, inv2, gain)).astype(BF)
    hidden_out = jnp.where(mine, h3, hidden_in[0])
    grad_in = jnp.where(mine, g1, cotangent[0])
    return (hidden_out[None], grad_in[None], shard[:3], shard[3].T)


def solution(mesh):
    grid = Mesh(mesh.devices.reshape(NP, 2, NN // 2, CTX // 2, 2), ("zp", "zq", "y") + CONTEXT)
    dp = ("zp", "zq", "y")
    in_specs = (
        P(dp, CONTEXT, None),
        P(dp, CONTEXT, None),
        P(dp, None),
        P(None, dp, CONTEXT),
        P(CONTEXT, dp),
        P(),
    )
    out_specs = (
        P(dp, CONTEXT, None),
        P(dp, CONTEXT, None),
        P(None, dp, CONTEXT),
        P(CONTEXT, dp),
    )
    return jax.shard_map(
        on_device, mesh=grid, in_specs=in_specs, out_specs=out_specs, check_vma=False
    )
```

```python
import jax
import jax.numpy as jnp
from jax import lax
from jax.sharding import Mesh, PartitionSpec as P

HD = 128
TILE = 128
D = 2048
CTX = 8
NP = 8
NN = 8
NEAR = ("zq", "y")
SCALE = HD**-0.5
CONTEXT = ("x", "core")
BF = jnp.bfloat16
F32 = jnp.float32


def swap(x, axis):
    return lax.all_to_all(x, axis, 0, 0)


def spread(x, axis, size):
    return swap(jnp.broadcast_to(x[None], (size,) + x.shape), axis)


def dot(a, b, dims):
    return lax.dot_general(a, b, (dims, ((), ())), preferred_element_type=F32)


def add(a, b):
    return (a.astype(F32) + b.astype(F32)).astype(BF)


def from_core(x):
    return lax.ppermute(x, "core", [(0, 1), (1, 0)])


def from_pair(x, bit):
    return lax.ppermute(x, "x", [(i, i ^ bit) for i in range(CTX // 2)])


def norm_chunk(x32, gain):
    inv = lax.rsqrt(jnp.mean(x32 * x32, -1, keepdims=True) + 1e-06)
    return inv, (x32 * inv * gain).astype(BF)


def core_half(x):
    low, high = x[: TILE // 2], x[TILE // 2 :]
    first = lax.axis_index("core") == 0
    return jnp.where(first, low, high), jnp.where(first, high, low)


def sum_half(terms):
    mine, other = core_half(terms)
    pair = add(mine, from_core(other))
    return jnp.sum(spread(pair, "x", CTX // 2).astype(F32), 0)


def both_halves(half):
    other = from_core(half)
    first = lax.axis_index("core") == 0
    return jnp.concatenate([jnp.where(first, half, other), jnp.where(first, other, half)], 0)


def forward(rows, w):
    q = dot(rows, w[0], ((1,), (0,))).astype(BF)
    k = dot(rows, w[1], ((1,), (0,))).astype(BF)
    v = dot(rows, w[2], ((1,), (0,))).astype(BF)
    pos = jnp.arange(TILE)
    scores = dot(q, k, ((1,), (1,))) * SCALE
    scores = jnp.where(pos[None, :] <= pos[:, None], scores, -1e30)
    expo = jnp.exp(scores - jnp.max(scores, -1, keepdims=True))
    prob = expo / jnp.sum(expo, -1, keepdims=True)
    probb = prob.astype(BF)
    attn = dot(probb, v, ((1,), (0,))).astype(BF)
    mixed = dot(attn, w[3], ((1,), (1,)))
    return mixed, (rows, q, k, v, prob, probb, attn)


def backward(dy, keep, w):
    rows, q, k, v, prob, probb, attn = keep
    dattn = dot(dy, w[3], ((1,), (0,))).astype(BF)
    delta = jnp.sum(dattn.astype(F32) * attn.astype(F32), -1, keepdims=True)
    dprob = dot(dattn, v, ((1,), (1,)))
    dscore = (prob * (dprob - delta) * SCALE).astype(BF)
    dq = dot(dscore, k, ((1,), (0,))).astype(BF)
    dk = dot(dscore, q, ((0,), (0,))).astype(BF)
    dv = dot(probb, dattn, ((0,), (0,))).astype(BF)
    return dq, dk, dv


def norm_terms(dqkv, w):
    dq, dk, dv = dqkv
    total = dot(dq, w[0], ((1,), (1,))) + dot(dk, w[1], ((1,), (1,))) + dot(dv, w[2], ((1,), (1,)))
    return total.astype(BF)


def norm_grad(e, x32, inv, gain):
    u = e * gain
    return inv * u - x32 * inv**3 * jnp.mean(x32 * u, -1, keepdims=True)


def on_device(hidden_in, cotangent, tile_depth, w_qkv, w_out, gain):
    me = lax.axis_index("x") * 2 + lax.axis_index("core")
    depth = tile_depth[0]
    places = jnp.arange(CTX, dtype=jnp.int32)
    alive = depth >= 2
    live3 = jnp.any(depth >= 3)
    mine = jnp.any(alive & (places == me))

    tokens = ((0,), (0,))
    core = lax.axis_index("core")
    none = jnp.zeros_like(hidden_in[0])
    shard = jnp.concatenate([w_qkv, w_out.T[None]], 0)
    shard, mine = lax.optimization_barrier((jnp.broadcast_to(shard[None], (NP,) + shard.shape), mine))
    near = swap(shard, "zp")
    h_part = jnp.where(mine, hidden_in[0], none)
    g_part = jnp.where(mine, cotangent[0], none)
    tile = jnp.where(core == 0, h_part, g_part) + from_core(jnp.where(core == 0, g_part, h_part))
    tile = tile + from_pair(tile, 1)

    near, tile = lax.optimization_barrier((near, tile))
    w = spread(near, NEAR, NN).transpose(2, 1, 0, 3, 4).reshape(4, D, HD)
    tile = tile + from_pair(tile, 3)
    other = from_core(tile)
    h1, g3 = jnp.where(core == 0, tile, other), jnp.where(core == 0, other, tile)

    x1 = h1.astype(F32)
    inv2, rows2 = norm_chunk(x1, gain)
    mixed2, keep2 = forward(rows2, w)
    attn2 = keep2[-1]
    h2 = both_halves((core_half(h1)[0].astype(F32) + sum_half(mixed2.astype(BF))).astype(BF))

    x2 = h2.astype(F32)
    inv3, normed3 = norm_chunk(x2, gain)
    rows3 = jnp.where(live3, normed3, jnp.zeros_like(normed3))
    dy3 = jnp.where(live3, g3, jnp.zeros_like(g3))
    mixed3, keep3 = forward(rows3, w)
    dqkv3 = backward(dy3, keep3, w)
    dnorm3, dqkv3 = lax.optimization_barrier((norm_terms(dqkv3, w), dqkv3))

    def products(rows, dqkv, dy, attn):
        terms = [dot(rows, d, tokens) for d in dqkv] + [dot(dy, attn, tokens)]
        return jnp.stack([x.reshape(NP, NN, 32, HD) for x in terms], 2)

    early = products(rows3, dqkv3, dy3, keep3[-1])
    x2c = core_half(h2)[0].astype(F32)
    inv3c, _ = norm_chunk(x2c, gain)
    g2c = core_half(g3)[0].astype(F32) + norm_grad(sum_half(dnorm3), x2c, inv3c, gain)
    g2c, early = lax.optimization_barrier((g2c.astype(BF), early))
    g2 = both_halves(g2c)

    dqkv2 = backward(g2, keep2, w)
    terms = (early + products(rows2, dqkv2, g2, attn2)).astype(BF).transpose(1, 0, 2, 3, 4)
    terms, dqkv2 = lax.optimization_barrier((terms, dqkv2))
    terms = swap(terms, NEAR)
    dnorm2 = norm_terms(dqkv2, w)

    mixed3 = mixed3.astype(BF)
    tile = add(jnp.where(core == 0, mixed3, dnorm2), from_core(jnp.where(core == 0, dnorm2, mixed3)))
    tile = add(tile, from_pair(tile, 1))
    terms, tile = lax.optimization_barrier((terms, tile))
    part = jnp.sum(terms.astype(F32), 0).astype(BF)
    shards = swap(part, "zp")

    tile = add(tile, from_pair(tile, 3))
    other = from_core(tile)
    sum3, sum2 = jnp.where(core == 0, tile, other), jnp.where(core == 0, other, tile)
    h3 = (x2 + sum3.astype(F32)).astype(BF)
    g1 = (g2.astype(F32) + norm_grad(sum2.astype(F32), x1, inv2, gain)).astype(BF)
    hidden_out = jnp.where(mine, h3, hidden_in[0])
    grad_in = jnp.where(mine, g1, cotangent[0])
    shard = jnp.sum(shards.astype(F32), 0)
    return (hidden_out[None], grad_in[None], shard[:3], shard[3].T)


def solution(mesh):
    grid = Mesh(mesh.devices.reshape(NP, 2, NN // 2, CTX // 2, 2), ("zp", "zq", "y") + CONTEXT)
    dp = ("zp", "zq", "y")
    in_specs = (
        P(dp, CONTEXT, None),
        P(dp, CONTEXT, None),
        P(dp, None),
        P(None, dp, CONTEXT),
        P(CONTEXT, dp),
        P(),
    )
    out_specs = (
        P(dp, CONTEXT, None),
        P(dp, CONTEXT, None),
        P(None, dp, CONTEXT),
        P(CONTEXT, dp),
    )
    return jax.shard_map(
        on_device, mesh=grid, in_specs=in_specs, out_specs=out_specs, check_vma=False
    )
```

```python
import jax
import jax.numpy as jnp
from jax import lax
from jax.experimental import pallas as pl
from jax.experimental.layout import Layout, with_layout_constraint
from jax.experimental.pallas import tpu as pltpu
from jax.sharding import Mesh, PartitionSpec as P

HD = 128
TILE = 128
D = 2048
CTX = 8
NP = 8
NN = 8
NEAR = ("zq", "y")
CHUNK = TILE // CTX
SCALE = HD**-0.5
CONTEXT = ("x", "core")
BF = jnp.bfloat16
F32 = jnp.float32


def swap(x, axis):
    return lax.all_to_all(x, axis, 0, 0)


def spread(x, axis, size):
    return swap(jnp.broadcast_to(x[None], (size,) + x.shape), axis)


def dot(a, b, dims):
    return lax.dot_general(a, b, (dims, ((), ())), preferred_element_type=F32)


def add(a, b):
    return (a.astype(F32) + b.astype(F32)).astype(BF)


def from_core(x):
    return lax.ppermute(x, "core", [(0, 1), (1, 0)])


def from_pair(x, bit):
    return lax.ppermute(x, "x", [(i, i ^ bit) for i in range(CTX // 2)])


def norm_chunk(x32, gain):
    inv = lax.rsqrt(jnp.mean(x32 * x32, -1, keepdims=True) + 1e-06)
    return inv, (x32 * inv * gain).astype(BF)


def all_rows(chunk):
    return lax.all_gather(chunk, CONTEXT, tiled=True)


def sum_chunk(terms):
    return jnp.sum(swap(terms.astype(BF).reshape(CTX, CHUNK, D), CONTEXT).astype(F32), 0)


def forward(rows, w):
    q = dot(rows, w[0], ((1,), (0,))).astype(BF)
    k = dot(rows, w[1], ((1,), (0,))).astype(BF)
    v = dot(rows, w[2], ((1,), (0,))).astype(BF)
    pos = jnp.arange(TILE)
    scores = dot(q, k, ((1,), (1,))) * SCALE
    scores = jnp.where(pos[None, :] <= pos[:, None], scores, -1e30)
    expo = jnp.exp(scores - jnp.max(scores, -1, keepdims=True))
    prob = expo / jnp.sum(expo, -1, keepdims=True)
    probb = prob.astype(BF)
    attn = dot(probb, v, ((1,), (0,))).astype(BF)
    mixed = dot(attn, w[3], ((1,), (1,)))
    return mixed, (rows, q, k, v, prob, probb, attn)


def backward(dy, keep, w):
    rows, q, k, v, prob, probb, attn = keep
    dattn = dot(dy, w[3], ((1,), (0,))).astype(BF)
    delta = jnp.sum(dattn.astype(F32) * attn.astype(F32), -1, keepdims=True)
    dprob = dot(dattn, v, ((1,), (1,)))
    dscore = (prob * (dprob - delta) * SCALE).astype(BF)
    dq = dot(dscore, k, ((1,), (0,))).astype(BF)
    dk = dot(dscore, q, ((0,), (0,))).astype(BF)
    dv = dot(probb, dattn, ((0,), (0,))).astype(BF)
    return dq, dk, dv


def norm_terms(dqkv, w):
    dq, dk, dv = dqkv
    total = dot(dq, w[0], ((1,), (1,))) + dot(dk, w[1], ((1,), (1,))) + dot(dv, w[2], ((1,), (1,)))
    return total.astype(BF)


def norm_grad(e, x32, inv, gain):
    u = e * gain
    return inv * u - x32 * inv**3 * jnp.mean(x32 * u, -1, keepdims=True)


def last_kernel(flags, tile, other, base_h, base_g, h1, inv, gain, out_h, out_g):
    first, mine = flags[0] == 0, flags[1] == 1
    a, b = tile[...].astype(F32), other[...].astype(F32)
    old_h, old_g = base_h[...], base_g[...]
    new_h = (old_h.astype(F32) + jnp.where(first, a, b)).astype(BF)
    dx = norm_grad(jnp.where(first, b, a), h1[...].astype(F32), inv[...], gain[...])
    new_g = (old_g.astype(F32) + dx).astype(BF)
    out_h[...] = jnp.where(mine, new_h, old_h)
    out_g[...] = jnp.where(mine, new_g, old_g)


def last_step(flags, tile, other, base_h, base_g, h1, inv, gain):
    steps = 4
    rows = pl.BlockSpec((TILE // steps, D), lambda i: (i, 0))
    return pl.pallas_call(
        last_kernel,
        grid=(steps,),
        in_specs=[pl.BlockSpec(memory_space=pltpu.SMEM)]
        + [rows] * 5
        + [pl.BlockSpec((TILE // steps, 1), lambda i: (i, 0)), pl.BlockSpec((1, D), lambda i: (0, 0))],
        out_specs=[rows, rows],
        out_shape=[jax.ShapeDtypeStruct((TILE, D), BF)] * 2,
        compiler_params=pltpu.CompilerParams(vmem_limit_bytes=16 * 2**20),
    )(flags, tile, other, base_h, base_g, h1, inv, gain.reshape(1, D))


def on_device(hidden_in, cotangent, tile_depth, w_qkv, w_out, gain):
    me = lax.axis_index("x") * 2 + lax.axis_index("core")
    depth = tile_depth[0]
    live3 = jnp.any(depth >= 3)
    mine = lax.dynamic_index_in_dim(depth, me, 0, keepdims=False) >= 2

    def chunk(tile):
        return lax.dynamic_index_in_dim(tile.reshape(CTX, CHUNK, D), me, 0, keepdims=False)

    tokens = ((0,), (0,))
    core = lax.axis_index("core")
    none = jnp.zeros_like(hidden_in[0])
    h_part = jnp.where(mine, hidden_in[0], none)
    g_part = jnp.where(mine, cotangent[0], none)
    tile = jnp.where(core == 0, h_part, g_part) + from_core(jnp.where(core == 0, g_part, h_part))
    tile = tile + from_pair(tile, 1)

    near = spread(jnp.concatenate([w_qkv, w_out.T[None]], 0), "zp", NP)
    near, tile = lax.optimization_barrier((near, tile))
    w = spread(near, NEAR, NN).transpose(2, 1, 0, 3, 4).reshape(4, D, HD)
    tile = tile + from_pair(tile, 3)
    other = from_core(tile)
    h1, g3 = jnp.where(core == 0, tile, other), jnp.where(core == 0, other, tile)

    x1 = h1.astype(F32)
    inv2, rows2 = norm_chunk(x1, gain)
    mixed2, keep2 = forward(rows2, w)
    attn2 = keep2[-1]
    h2c = (chunk(h1).astype(F32) + sum_chunk(mixed2)).astype(BF)
    h2 = all_rows(h2c)

    x2 = h2.astype(F32)
    inv3, normed3 = norm_chunk(x2, gain)
    rows3 = jnp.where(live3, normed3, jnp.zeros_like(normed3))
    dy3 = jnp.where(live3, g3, jnp.zeros_like(g3))
    rows3 = lax.optimization_barrier(rows3)
    mixed3, keep3 = forward(rows3, w)
    dqkv3 = backward(dy3, keep3, w)
    dnorm3 = norm_terms(dqkv3, w)
    x2c = chunk(h2).astype(F32)
    inv3c, _ = norm_chunk(x2c, gain)
    g2c = chunk(g3).astype(F32) + norm_grad(sum_chunk(dnorm3), x2c, inv3c, gain)
    g2 = all_rows(g2c.astype(BF))

    dqkv2 = backward(g2, keep2, w)

    def product(left3, right3, left2, right2):
        both = dot(jnp.concatenate([left3, left2], 0), jnp.concatenate([right3, right2], 0), tokens)
        return both.astype(BF).reshape(NP, NN, 32, HD)

    terms = [product(rows3, d3, rows2, d2) for d3, d2 in zip(dqkv3, dqkv2)]
    terms.append(product(dy3, keep3[-1], g2, attn2))
    terms = jnp.stack(terms, 2).transpose(1, 0, 2, 3, 4)
    terms = with_layout_constraint(terms, Layout((0, 1, 2, 3, 4)))
    terms, dqkv2, old_h, old_g = lax.optimization_barrier((terms, dqkv2, h2, g2))
    terms = swap(terms, NEAR)
    base_h = jnp.where(mine, old_h, hidden_in[0])
    base_g = jnp.where(mine, old_g, cotangent[0])
    dnorm2 = norm_terms(dqkv2, w)

    mixed3 = mixed3.astype(BF)
    tile = add(jnp.where(core == 0, mixed3, dnorm2), from_core(jnp.where(core == 0, dnorm2, mixed3)))
    tile = add(tile, from_pair(tile, 1))
    terms, tile, base_h, base_g = lax.optimization_barrier((terms, tile, base_h, base_g))

    part = jnp.sum(terms.astype(F32), 0).astype(BF)
    shard = jnp.sum(swap(part, "zp").astype(F32), 0)

    tile = add(tile, from_pair(tile, 3))
    other = from_core(tile)
    flags = jnp.stack([core, mine.astype(jnp.int32)])
    hidden_out, grad_in = last_step(flags, tile, other, base_h, base_g, h1, inv2, gain)
    return (hidden_out[None], grad_in[None], shard[:3], shard[3].T)


def solution(mesh):
    grid = Mesh(mesh.devices.reshape(NP, 2, NN // 2, CTX // 2, 2), ("zp", "zq", "y") + CONTEXT)
    dp = ("zp", "zq", "y")
    in_specs = (
        P(dp, CONTEXT, None),
        P(dp, CONTEXT, None),
        P(dp, None),
        P(None, dp, CONTEXT),
        P(CONTEXT, dp),
        P(),
    )
    out_specs = (
        P(dp, CONTEXT, None),
        P(dp, CONTEXT, None),
        P(None, dp, CONTEXT),
        P(CONTEXT, dp),
    )
    return jax.shard_map(
        on_device, mesh=grid, in_specs=in_specs, out_specs=out_specs, check_vma=False
    )
```

```python
import jax
import jax.numpy as jnp
from jax import lax
from jax.experimental import pallas as pl
from jax.experimental.layout import Layout, with_layout_constraint
from jax.experimental.pallas import tpu as pltpu
from jax.sharding import Mesh, PartitionSpec as P

HD = 128
TILE = 128
D = 2048
CTX = 8
NP = 8
NN = 8
NEAR = ("zq", "y")
CHUNK = TILE // CTX
SCALE = HD**-0.5
CONTEXT = ("x", "core")
BF = jnp.bfloat16
F32 = jnp.float32


def swap(x, axis):
    return lax.all_to_all(x, axis, 0, 0)


def spread(x, axis, size):
    return swap(jnp.broadcast_to(x[None], (size,) + x.shape), axis)


def dot(a, b, dims):
    return lax.dot_general(a, b, (dims, ((), ())), preferred_element_type=F32)


def add(a, b):
    return (a.astype(F32) + b.astype(F32)).astype(BF)


def from_core(x):
    return lax.ppermute(x, "core", [(0, 1), (1, 0)])


def from_pair(x, bit):
    return lax.ppermute(x, "x", [(i, i ^ bit) for i in range(CTX // 2)])


def norm_chunk(x32, gain):
    inv = lax.rsqrt(jnp.mean(x32 * x32, -1, keepdims=True) + 1e-06)
    return inv, (x32 * inv * gain).astype(BF)


def all_rows(chunk):
    return lax.all_gather(chunk, CONTEXT, tiled=True)


def sum_chunk(terms):
    return jnp.sum(swap(terms.astype(BF).reshape(CTX, CHUNK, D), CONTEXT).astype(F32), 0)


def forward(rows, w):
    q = dot(rows, w[0], ((1,), (0,))).astype(BF)
    k = dot(rows, w[1], ((1,), (0,))).astype(BF)
    v = dot(rows, w[2], ((1,), (0,))).astype(BF)
    pos = jnp.arange(TILE)
    scores = dot(q, k, ((1,), (1,))) * SCALE
    scores = jnp.where(pos[None, :] <= pos[:, None], scores, -1e30)
    expo = jnp.exp(scores - jnp.max(scores, -1, keepdims=True))
    prob = expo / jnp.sum(expo, -1, keepdims=True)
    probb = prob.astype(BF)
    attn = dot(probb, v, ((1,), (0,))).astype(BF)
    mixed = dot(attn, w[3], ((1,), (1,)))
    return mixed, (rows, q, k, v, prob, probb, attn)


def backward(dy, keep, w):
    rows, q, k, v, prob, probb, attn = keep
    dattn = dot(dy, w[3], ((1,), (0,))).astype(BF)
    delta = jnp.sum(dattn.astype(F32) * attn.astype(F32), -1, keepdims=True)
    dprob = dot(dattn, v, ((1,), (1,)))
    dscore = (prob * (dprob - delta) * SCALE).astype(BF)
    dq = dot(dscore, k, ((1,), (0,))).astype(BF)
    dk = dot(dscore, q, ((0,), (0,))).astype(BF)
    dv = dot(probb, dattn, ((0,), (0,))).astype(BF)
    return dq, dk, dv


def norm_terms(dqkv, w):
    dq, dk, dv = dqkv
    total = dot(dq, w[0], ((1,), (1,))) + dot(dk, w[1], ((1,), (1,))) + dot(dv, w[2], ((1,), (1,)))
    return total.astype(BF)


def norm_grad(e, x32, inv, gain):
    u = e * gain
    return inv * u - x32 * inv**3 * jnp.mean(x32 * u, -1, keepdims=True)


def last_kernel(flags, tile, other, base_h, base_g, h1, inv, gain, out_h, out_g):
    first, mine = flags[0] == 0, flags[1] == 1
    a, b = tile[...].astype(F32), other[...].astype(F32)
    old_h, old_g = base_h[...], base_g[...]
    new_h = (old_h.astype(F32) + jnp.where(first, a, b)).astype(BF)
    dx = norm_grad(jnp.where(first, b, a), h1[...].astype(F32), inv[...], gain[...])
    new_g = (old_g.astype(F32) + dx).astype(BF)
    out_h[...] = jnp.where(mine, new_h, old_h)
    out_g[...] = jnp.where(mine, new_g, old_g)


def last_step(flags, tile, other, base_h, base_g, h1, inv, gain):
    steps = 4
    rows = pl.BlockSpec((TILE // steps, D), lambda i: (i, 0))
    return pl.pallas_call(
        last_kernel,
        grid=(steps,),
        in_specs=[pl.BlockSpec(memory_space=pltpu.SMEM)]
        + [rows] * 5
        + [pl.BlockSpec((TILE // steps, 1), lambda i: (i, 0)), pl.BlockSpec((1, D), lambda i: (0, 0))],
        out_specs=[rows, rows],
        out_shape=[jax.ShapeDtypeStruct((TILE, D), BF)] * 2,
        compiler_params=pltpu.CompilerParams(vmem_limit_bytes=16 * 2**20),
    )(flags, tile, other, base_h, base_g, h1, inv, gain.reshape(1, D))


def on_device(hidden_in, cotangent, tile_depth, w_qkv, w_out, gain):
    me = lax.axis_index("x") * 2 + lax.axis_index("core")
    depth = tile_depth[0]
    live3 = jnp.any(depth >= 3)
    mine = lax.dynamic_index_in_dim(depth, me, 0, keepdims=False) >= 2

    def chunk(tile):
        return lax.dynamic_index_in_dim(tile.reshape(CTX, CHUNK, D), me, 0, keepdims=False)

    tokens = ((0,), (0,))
    core = lax.axis_index("core")
    none = jnp.zeros_like(hidden_in[0])
    h_part = jnp.where(mine, hidden_in[0], none)
    g_part = jnp.where(mine, cotangent[0], none)
    tile = jnp.where(core == 0, h_part, g_part) + from_core(jnp.where(core == 0, g_part, h_part))
    tile = tile + from_pair(tile, 1)

    near = lax.all_gather(jnp.concatenate([w_qkv, w_out.T[None]], 0), "zp")
    near, tile = lax.optimization_barrier((near, tile))
    w = spread(near, NEAR, NN).transpose(2, 1, 0, 3, 4).reshape(4, D, HD)
    tile = tile + from_pair(tile, 3)
    other = from_core(tile)
    h1, g3 = jnp.where(core == 0, tile, other), jnp.where(core == 0, other, tile)

    x1 = h1.astype(F32)
    inv2, rows2 = norm_chunk(x1, gain)
    mixed2, keep2 = forward(rows2, w)
    attn2 = keep2[-1]
    h2c = (chunk(h1).astype(F32) + sum_chunk(mixed2)).astype(BF)
    h2 = all_rows(h2c)

    x2 = h2.astype(F32)
    inv3, normed3 = norm_chunk(x2, gain)
    rows3 = jnp.where(live3, normed3, jnp.zeros_like(normed3))
    dy3 = jnp.where(live3, g3, jnp.zeros_like(g3))
    rows3 = lax.optimization_barrier(rows3)
    mixed3, keep3 = forward(rows3, w)
    dqkv3 = backward(dy3, keep3, w)
    dnorm3 = norm_terms(dqkv3, w)
    x2c = chunk(h2).astype(F32)
    inv3c, _ = norm_chunk(x2c, gain)
    g2c = chunk(g3).astype(F32) + norm_grad(sum_chunk(dnorm3), x2c, inv3c, gain)
    g2 = all_rows(g2c.astype(BF))

    dqkv2 = backward(g2, keep2, w)

    def product(left3, right3, left2, right2):
        both = dot(jnp.concatenate([left3, left2], 0), jnp.concatenate([right3, right2], 0), tokens)
        return both.astype(BF).reshape(NP, NN, 32, HD)

    terms = [product(rows3, d3, rows2, d2) for d3, d2 in zip(dqkv3, dqkv2)]
    terms.append(product(dy3, keep3[-1], g2, attn2))
    terms = jnp.stack(terms, 2).transpose(1, 0, 2, 3, 4)
    terms = with_layout_constraint(terms, Layout((0, 1, 2, 3, 4)))
    terms, dqkv2, old_h, old_g = lax.optimization_barrier((terms, dqkv2, h2, g2))
    terms = swap(terms, NEAR)
    base_h = jnp.where(mine, old_h, hidden_in[0])
    base_g = jnp.where(mine, old_g, cotangent[0])
    dnorm2 = norm_terms(dqkv2, w)

    mixed3 = mixed3.astype(BF)
    tile = add(jnp.where(core == 0, mixed3, dnorm2), from_core(jnp.where(core == 0, dnorm2, mixed3)))
    tile = add(tile, from_pair(tile, 1))
    terms, tile, base_h, base_g = lax.optimization_barrier((terms, tile, base_h, base_g))

    part = jnp.sum(terms.astype(F32), 0).astype(BF)
    shards = swap(part, "zp")

    tile = add(tile, from_pair(tile, 3))
    other = from_core(tile)
    flags = jnp.stack([core, mine.astype(jnp.int32)])
    hidden_out, grad_in = last_step(flags, tile, other, base_h, base_g, h1, inv2, gain)
    shards, hidden_out, grad_in = lax.optimization_barrier((shards, hidden_out, grad_in))
    shard = jnp.sum(shards.astype(F32), 0)
    return (hidden_out[None], grad_in[None], shard[:3], shard[3].T)


def solution(mesh):
    grid = Mesh(mesh.devices.reshape(NP, 2, NN // 2, CTX // 2, 2), ("zp", "zq", "y") + CONTEXT)
    dp = ("zp", "zq", "y")
    in_specs = (
        P(dp, CONTEXT, None),
        P(dp, CONTEXT, None),
        P(dp, None),
        P(None, dp, CONTEXT),
        P(CONTEXT, dp),
        P(),
    )
    out_specs = (
        P(dp, CONTEXT, None),
        P(dp, CONTEXT, None),
        P(None, dp, CONTEXT),
        P(CONTEXT, dp),
    )
    return jax.shard_map(
        on_device, mesh=grid, in_specs=in_specs, out_specs=out_specs, check_vma=False
    )
```

```python
import jax
import jax.numpy as jnp
from jax import lax
from jax.experimental import pallas as pl
from jax.experimental.layout import Layout, with_layout_constraint
from jax.experimental.pallas import tpu as pltpu
from jax.sharding import Mesh, PartitionSpec as P

HD = 128
TILE = 128
D = 2048
CTX = 8
NP = 8
NN = 8
NEAR = ("zq", "y")
CHUNK = TILE // CTX
SCALE = HD**-0.5
CONTEXT = ("x", "core")
BF = jnp.bfloat16
F32 = jnp.float32


def swap(x, axis):
    return lax.all_to_all(x, axis, 0, 0)


def spread(x, axis, size):
    return swap(jnp.broadcast_to(x[None], (size,) + x.shape), axis)


def dot(a, b, dims):
    return lax.dot_general(a, b, (dims, ((), ())), preferred_element_type=F32)


def add(a, b):
    return (a.astype(F32) + b.astype(F32)).astype(BF)


def from_core(x):
    return lax.ppermute(x, "core", [(0, 1), (1, 0)])


def from_pair(x, bit):
    return lax.ppermute(x, "x", [(i, i ^ bit) for i in range(CTX // 2)])


def norm_chunk(x32, gain):
    inv = lax.rsqrt(jnp.mean(x32 * x32, -1, keepdims=True) + 1e-06)
    return inv, (x32 * inv * gain).astype(BF)


def all_rows(chunk):
    return lax.all_gather(chunk, CONTEXT, tiled=True)


def sum_chunk(terms):
    return jnp.sum(swap(terms.astype(BF).reshape(CTX, CHUNK, D), CONTEXT).astype(F32), 0)


def forward(rows, w):
    q = dot(rows, w[0], ((1,), (0,))).astype(BF)
    k = dot(rows, w[1], ((1,), (0,))).astype(BF)
    v = dot(rows, w[2], ((1,), (0,))).astype(BF)
    pos = jnp.arange(TILE)
    scores = dot(q, k, ((1,), (1,))) * SCALE
    scores = jnp.where(pos[None, :] <= pos[:, None], scores, -1e30)
    expo = jnp.exp(scores - jnp.max(scores, -1, keepdims=True))
    prob = expo / jnp.sum(expo, -1, keepdims=True)
    probb = prob.astype(BF)
    attn = dot(probb, v, ((1,), (0,))).astype(BF)
    mixed = dot(attn, w[3], ((1,), (1,)))
    return mixed, (rows, q, k, v, prob, probb, attn)


def backward(dy, keep, w):
    rows, q, k, v, prob, probb, attn = keep
    dattn = dot(dy, w[3], ((1,), (0,))).astype(BF)
    delta = jnp.sum(dattn.astype(F32) * attn.astype(F32), -1, keepdims=True)
    dprob = dot(dattn, v, ((1,), (1,)))
    dscore = (prob * (dprob - delta) * SCALE).astype(BF)
    dq = dot(dscore, k, ((1,), (0,))).astype(BF)
    dk = dot(dscore, q, ((0,), (0,))).astype(BF)
    dv = dot(probb, dattn, ((0,), (0,))).astype(BF)
    return dq, dk, dv


def norm_terms(dqkv, w):
    dq, dk, dv = dqkv
    total = dot(dq, w[0], ((1,), (1,))) + dot(dk, w[1], ((1,), (1,))) + dot(dv, w[2], ((1,), (1,)))
    return total.astype(BF)


def norm_grad(e, x32, inv, gain):
    u = e * gain
    return inv * u - x32 * inv**3 * jnp.mean(x32 * u, -1, keepdims=True)


def first_kernel(places, depth, h, g, w_qkv, w_out, sent, shards):
    first, live = places[0] == 0, depth[0, places[1]] >= 2
    tile = jnp.where(first, g[...], h[...])
    sent[...] = jnp.where(live, tile, jnp.zeros_like(tile))
    for i in range(NP):
        shards[i, :3] = w_qkv[...]
        shards[i, 3] = w_out[...]


def first_step(places, depth, h, g, w_qkv, w_out):
    scalars = pl.BlockSpec(memory_space=pltpu.SMEM)
    return pl.pallas_call(
        first_kernel,
        in_specs=[scalars, scalars] + [pl.BlockSpec(memory_space=pltpu.VMEM)] * 4,
        out_specs=[pl.BlockSpec(memory_space=pltpu.VMEM)] * 2,
        out_shape=[
            jax.ShapeDtypeStruct((TILE, D), BF),
            jax.ShapeDtypeStruct((NP, 4, 32, HD), BF),
        ],
        compiler_params=pltpu.CompilerParams(vmem_limit_bytes=16 * 2**20),
    )(places, depth, h, g, w_qkv, w_out)


def copies_kernel(near, out):
    for t in range(4):
        out[0, t] = near[:, t]


def copies(near):
    return pl.pallas_call(
        copies_kernel,
        grid=(NN,),
        in_specs=[pl.BlockSpec((NP, 4, 32, HD), lambda i: (0, 0, 0, 0))],
        out_specs=pl.BlockSpec((1, 4, NP, 32, HD), lambda i: (i, 0, 0, 0, 0)),
        out_shape=jax.ShapeDtypeStruct((NN, 4, NP, 32, HD), BF),
        compiler_params=pltpu.CompilerParams(vmem_limit_bytes=16 * 2**20),
    )(near)


def sum_kernel(terms, out):
    total = terms[0].astype(F32)
    for i in range(1, NN):
        total = total + terms[i].astype(F32)
    out[...] = total.astype(BF)


def sum_terms(terms):
    return pl.pallas_call(
        sum_kernel,
        grid=(NP // 2,),
        in_specs=[pl.BlockSpec((NN, 2, 4, 32, HD), lambda i: (0, i, 0, 0, 0))],
        out_specs=pl.BlockSpec((2, 4, 32, HD), lambda i: (i, 0, 0, 0)),
        out_shape=jax.ShapeDtypeStruct((NP, 4, 32, HD), BF),
        compiler_params=pltpu.CompilerParams(vmem_limit_bytes=16 * 2**20),
    )(terms)


def shards_kernel(terms, qkv, out):
    total = terms[0].astype(F32)
    for i in range(1, NP):
        total = total + terms[i].astype(F32)
    qkv[...] = total[:3]
    out[...] = total[3]


def weight_shards(terms):
    return pl.pallas_call(
        shards_kernel,
        out_shape=[
            jax.ShapeDtypeStruct((3, 32, HD), F32),
            jax.ShapeDtypeStruct((32, HD), F32),
        ],
    )(terms)


def last_kernel(flags, tile, other, base_h, base_g, h1, inv, gain, out_h, out_g):
    first, mine = flags[0] == 0, flags[1] == 1
    a, b = tile[...].astype(F32), other[...].astype(F32)
    old_h, old_g = base_h[...], base_g[...]
    new_h = (old_h.astype(F32) + jnp.where(first, a, b)).astype(BF)
    dx = norm_grad(jnp.where(first, b, a), h1[...].astype(F32), inv[...], gain[...])
    new_g = (old_g.astype(F32) + dx).astype(BF)
    out_h[...] = jnp.where(mine, new_h, old_h)
    out_g[...] = jnp.where(mine, new_g, old_g)


def last_step(flags, tile, other, base_h, base_g, h1, inv, gain):
    steps = 4
    rows = pl.BlockSpec((TILE // steps, D), lambda i: (i, 0))
    return pl.pallas_call(
        last_kernel,
        grid=(steps,),
        in_specs=[pl.BlockSpec(memory_space=pltpu.SMEM)]
        + [rows] * 5
        + [pl.BlockSpec((TILE // steps, 1), lambda i: (i, 0)), pl.BlockSpec((1, D), lambda i: (0, 0))],
        out_specs=[rows, rows],
        out_shape=[jax.ShapeDtypeStruct((TILE, D), BF)] * 2,
        compiler_params=pltpu.CompilerParams(vmem_limit_bytes=16 * 2**20),
    )(flags, tile, other, base_h, base_g, h1, inv, gain.reshape(1, D))


def on_device(hidden_in, cotangent, tile_depth, w_qkv, w_out, gain):
    me = lax.axis_index("x") * 2 + lax.axis_index("core")
    depth = tile_depth[0]
    live3 = jnp.any(depth >= 3)
    mine = lax.dynamic_index_in_dim(depth, me, 0, keepdims=False) >= 2

    def chunk(tile):
        return lax.dynamic_index_in_dim(tile.reshape(CTX, CHUNK, D), me, 0, keepdims=False)

    tokens = ((0,), (0,))
    core = lax.axis_index("core")
    none = jnp.zeros_like(hidden_in[0])
    places = jnp.stack([core, me])
    sent, shards = first_step(places, tile_depth, hidden_in[0], cotangent[0], w_qkv, w_out.T)
    kept = jnp.where(mine, jnp.where(core == 0, hidden_in[0], cotangent[0]), none)
    tile = kept + from_core(sent)
    tile = tile + from_pair(tile, 1)

    near = swap(shards, "zp")
    near, tile = lax.optimization_barrier((near, tile))
    w = swap(copies(near), NEAR).transpose(1, 2, 0, 3, 4).reshape(4, D, HD)
    tile = tile + from_pair(tile, 3)
    other = from_core(tile)
    h1, g3 = jnp.where(core == 0, tile, other), jnp.where(core == 0, other, tile)

    x1 = h1.astype(F32)
    inv2, rows2 = norm_chunk(x1, gain)
    mixed2, keep2 = forward(rows2, w)
    attn2 = keep2[-1]
    h2c = (chunk(h1).astype(F32) + sum_chunk(mixed2)).astype(BF)
    h2 = all_rows(h2c)

    x2 = h2.astype(F32)
    inv3, normed3 = norm_chunk(x2, gain)
    rows3 = jnp.where(live3, normed3, jnp.zeros_like(normed3))
    dy3 = jnp.where(live3, g3, jnp.zeros_like(g3))
    rows3 = lax.optimization_barrier(rows3)
    mixed3, keep3 = forward(rows3, w)
    dqkv3 = backward(dy3, keep3, w)
    dnorm3 = norm_terms(dqkv3, w)
    x2c = chunk(h2).astype(F32)
    inv3c, _ = norm_chunk(x2c, gain)
    g2c = chunk(g3).astype(F32) + norm_grad(sum_chunk(dnorm3), x2c, inv3c, gain)
    g2 = all_rows(g2c.astype(BF))

    dqkv2 = backward(g2, keep2, w)

    def product(left3, right3, left2, right2):
        both = dot(jnp.concatenate([left3, left2], 0), jnp.concatenate([right3, right2], 0), tokens)
        return both.astype(BF).reshape(NP, NN, 32, HD)

    terms = [product(rows3, d3, rows2, d2) for d3, d2 in zip(dqkv3, dqkv2)]
    terms.append(product(dy3, keep3[-1], g2, attn2))
    terms = jnp.stack(terms, 2).transpose(1, 0, 2, 3, 4)
    terms = with_layout_constraint(terms, Layout((0, 1, 2, 3, 4)))
    terms, dqkv2, old_h, old_g = lax.optimization_barrier((terms, dqkv2, h2, g2))
    terms = swap(terms, NEAR)
    base_h = jnp.where(mine, old_h, hidden_in[0])
    base_g = jnp.where(mine, old_g, cotangent[0])
    dnorm2 = norm_terms(dqkv2, w)

    mixed3 = mixed3.astype(BF)
    tile = add(jnp.where(core == 0, mixed3, dnorm2), from_core(jnp.where(core == 0, dnorm2, mixed3)))
    tile = add(tile, from_pair(tile, 1))
    pair = from_pair(tile, 3)

    part = sum_terms(terms)
    shards = swap(part, "zp")

    tile, pair, _ = lax.optimization_barrier((tile, pair, part))
    tile = add(tile, pair)
    other = from_core(tile)
    flags = jnp.stack([core, mine.astype(jnp.int32)])
    hidden_out, grad_in = last_step(flags, tile, other, base_h, base_g, h1, inv2, gain)
    shards, hidden_out, grad_in = lax.optimization_barrier((shards, hidden_out, grad_in))
    grad_qkv, grad_out = weight_shards(shards)
    return (hidden_out[None], grad_in[None], grad_qkv, grad_out.T)


def solution(mesh):
    grid = Mesh(mesh.devices.reshape(NP, 2, NN // 2, CTX // 2, 2), ("zp", "zq", "y") + CONTEXT)
    dp = ("zp", "zq", "y")
    in_specs = (
        P(dp, CONTEXT, None),
        P(dp, CONTEXT, None),
        P(dp, None),
        P(None, dp, CONTEXT),
        P(CONTEXT, dp),
        P(),
    )
    out_specs = (
        P(dp, CONTEXT, None),
        P(dp, CONTEXT, None),
        P(None, dp, CONTEXT),
        P(CONTEXT, dp),
    )
    return jax.shard_map(
        on_device, mesh=grid, in_specs=in_specs, out_specs=out_specs, check_vma=False
    )
```

```python
import jax
import jax.numpy as jnp
from jax import lax
from jax.experimental import pallas as pl
from jax.experimental.layout import Layout, with_layout_constraint
from jax.experimental.pallas import tpu as pltpu
from jax.sharding import Mesh, PartitionSpec as P

HD = 128
TILE = 128
D = 2048
CTX = 8
NP = 8
NN = 8
NEAR = ("zq", "y")
CHUNK = TILE // CTX
SCALE = HD**-0.5
CONTEXT = ("x", "core")
BF = jnp.bfloat16
F32 = jnp.float32


def swap(x, axis):
    return lax.all_to_all(x, axis, 0, 0)


def spread(x, axis, size):
    return swap(jnp.broadcast_to(x[None], (size,) + x.shape), axis)


def dot(a, b, dims):
    return lax.dot_general(a, b, (dims, ((), ())), preferred_element_type=F32)


def add(a, b):
    return (a.astype(F32) + b.astype(F32)).astype(BF)


def from_core(x):
    return lax.ppermute(x, "core", [(0, 1), (1, 0)])


def from_pair(x, bit):
    return lax.ppermute(x, "x", [(i, i ^ bit) for i in range(CTX // 2)])


def norm_chunk(x32, gain):
    inv = lax.rsqrt(jnp.mean(x32 * x32, -1, keepdims=True) + 1e-06)
    return inv, (x32 * inv * gain).astype(BF)


def all_rows(chunk):
    return lax.all_gather(chunk, CONTEXT, tiled=True)


def sum_chunk(terms):
    return jnp.sum(swap(terms.astype(BF).reshape(CTX, CHUNK, D), CONTEXT).astype(F32), 0)


def forward(rows, w):
    q = dot(rows, w[0], ((1,), (0,))).astype(BF)
    k = dot(rows, w[1], ((1,), (0,))).astype(BF)
    v = dot(rows, w[2], ((1,), (0,))).astype(BF)
    pos = jnp.arange(TILE)
    scores = dot(q, k, ((1,), (1,))) * SCALE
    scores = jnp.where(pos[None, :] <= pos[:, None], scores, -1e30)
    expo = jnp.exp(scores - jnp.max(scores, -1, keepdims=True))
    prob = expo / jnp.sum(expo, -1, keepdims=True)
    probb = prob.astype(BF)
    attn = dot(probb, v, ((1,), (0,))).astype(BF)
    mixed = dot(attn, w[3], ((1,), (1,)))
    return mixed, (rows, q, k, v, prob, probb, attn)


def backward(dy, keep, w):
    rows, q, k, v, prob, probb, attn = keep
    dattn = dot(dy, w[3], ((1,), (0,))).astype(BF)
    delta = jnp.sum(dattn.astype(F32) * attn.astype(F32), -1, keepdims=True)
    dprob = dot(dattn, v, ((1,), (1,)))
    dscore = (prob * (dprob - delta) * SCALE).astype(BF)
    dq = dot(dscore, k, ((1,), (0,))).astype(BF)
    dk = dot(dscore, q, ((0,), (0,))).astype(BF)
    dv = dot(probb, dattn, ((0,), (0,))).astype(BF)
    return dq, dk, dv


def norm_terms(dqkv, w):
    dq, dk, dv = dqkv
    total = dot(dq, w[0], ((1,), (1,))) + dot(dk, w[1], ((1,), (1,))) + dot(dv, w[2], ((1,), (1,)))
    return total.astype(BF)


def norm_grad(e, x32, inv, gain):
    u = e * gain
    return inv * u - x32 * inv**3 * jnp.mean(x32 * u, -1, keepdims=True)


def first_kernel(depth, h, g, w_qkv, w_out, sent, shards, qkv_in, out_in, sems):
    core = lax.axis_index("core")
    live = depth[0, lax.axis_index("x") * 2 + core] >= 2
    weights = [
        pltpu.make_async_copy(w_qkv, qkv_in, sems.at[0]),
        pltpu.make_async_copy(w_out, out_in, sems.at[1]),
    ]
    for copy in weights:
        copy.start()

    @pl.when(live & (core == 0))
    def _():
        copy = pltpu.make_async_copy(g, sent, sems.at[2])
        copy.start()
        copy.wait()

    @pl.when(live & (core == 1))
    def _():
        copy = pltpu.make_async_copy(h, sent, sems.at[3])
        copy.start()
        copy.wait()

    @pl.when(jnp.logical_not(live))
    def _():
        sent[...] = jnp.zeros_like(sent)

    for copy in weights:
        copy.wait()
    for i in range(NP):
        shards[i, :3] = qkv_in[...]
        shards[i, 3] = out_in[...]


def first_step(depth, h, g, w_qkv, w_out):
    return pl.pallas_call(
        first_kernel,
        in_specs=[pl.BlockSpec(memory_space=pltpu.SMEM)] + [pl.BlockSpec(memory_space=pl.ANY)] * 4,
        out_specs=[pl.BlockSpec(memory_space=pltpu.VMEM)] * 2,
        out_shape=[
            jax.ShapeDtypeStruct((TILE, D), BF),
            jax.ShapeDtypeStruct((NP, 4, 32, HD), BF),
        ],
        scratch_shapes=[
            pltpu.VMEM((3, 32, HD), BF),
            pltpu.VMEM((32, HD), BF),
            pltpu.SemaphoreType.DMA((4,)),
        ],
        compiler_params=pltpu.CompilerParams(vmem_limit_bytes=60 * 2**20),
    )(depth, h, g, w_qkv, w_out)


def sum_kernel(terms, out):
    total = terms[0].astype(F32)
    for i in range(1, NN):
        total = total + terms[i].astype(F32)
    out[...] = total.astype(BF)


def sum_terms(terms):
    return pl.pallas_call(
        sum_kernel,
        grid=(NP // 2,),
        in_specs=[pl.BlockSpec((NN, 2, 4, 32, HD), lambda i: (0, i, 0, 0, 0))],
        out_specs=pl.BlockSpec((2, 4, 32, HD), lambda i: (i, 0, 0, 0)),
        out_shape=jax.ShapeDtypeStruct((NP, 4, 32, HD), BF),
        compiler_params=pltpu.CompilerParams(vmem_limit_bytes=16 * 2**20),
    )(terms)


def last_kernel(flags, tile, other, base_h, base_g, h1, inv, gain, out_h, out_g):
    first, mine = flags[0] == 0, flags[1] == 1
    a, b = tile[...].astype(F32), other[...].astype(F32)
    old_h, old_g = base_h[...], base_g[...]
    new_h = (old_h.astype(F32) + jnp.where(first, a, b)).astype(BF)
    dx = norm_grad(jnp.where(first, b, a), h1[...].astype(F32), inv[...], gain[...])
    new_g = (old_g.astype(F32) + dx).astype(BF)
    out_h[...] = jnp.where(mine, new_h, old_h)
    out_g[...] = jnp.where(mine, new_g, old_g)


def last_step(flags, tile, other, base_h, base_g, h1, inv, gain):
    steps = 4
    rows = pl.BlockSpec((TILE // steps, D), lambda i: (i, 0))
    return pl.pallas_call(
        last_kernel,
        grid=(steps,),
        in_specs=[pl.BlockSpec(memory_space=pltpu.SMEM)]
        + [rows] * 5
        + [pl.BlockSpec((TILE // steps, 1), lambda i: (i, 0)), pl.BlockSpec((1, D), lambda i: (0, 0))],
        out_specs=[rows, rows],
        out_shape=[jax.ShapeDtypeStruct((TILE, D), BF)] * 2,
        compiler_params=pltpu.CompilerParams(vmem_limit_bytes=16 * 2**20),
    )(flags, tile, other, base_h, base_g, h1, inv, gain.reshape(1, D))


def on_device(hidden_in, cotangent, tile_depth, w_qkv, w_out, gain):
    me = lax.axis_index("x") * 2 + lax.axis_index("core")
    depth = tile_depth[0]
    live3 = jnp.any(depth >= 3)
    mine = lax.dynamic_index_in_dim(depth, me, 0, keepdims=False) >= 2

    def chunk(tile):
        return lax.dynamic_index_in_dim(tile.reshape(CTX, CHUNK, D), me, 0, keepdims=False)

    tokens = ((0,), (0,))
    core = lax.axis_index("core")
    none = jnp.zeros_like(hidden_in[0])
    sent, shards = first_step(tile_depth, hidden_in[0], cotangent[0], w_qkv, w_out.T)
    kept = jnp.where(mine, jnp.where(core == 0, hidden_in[0], cotangent[0]), none)
    tile = kept + from_core(sent)
    tile = tile + from_pair(tile, 1)

    near = swap(shards, "zp")
    near, tile = lax.optimization_barrier((near, tile))
    w = spread(near, NEAR, NN).transpose(2, 1, 0, 3, 4).reshape(4, D, HD)
    tile = tile + from_pair(tile, 3)
    other = from_core(tile)
    h1, g3 = jnp.where(core == 0, tile, other), jnp.where(core == 0, other, tile)

    x1 = h1.astype(F32)
    inv2, rows2 = norm_chunk(x1, gain)
    mixed2, keep2 = forward(rows2, w)
    attn2 = keep2[-1]
    h2c = (chunk(h1).astype(F32) + sum_chunk(mixed2)).astype(BF)
    h2 = all_rows(h2c)

    x2 = h2.astype(F32)
    inv3, normed3 = norm_chunk(x2, gain)
    rows3 = jnp.where(live3, normed3, jnp.zeros_like(normed3))
    dy3 = jnp.where(live3, g3, jnp.zeros_like(g3))
    rows3 = lax.optimization_barrier(rows3)
    mixed3, keep3 = forward(rows3, w)
    dqkv3 = backward(dy3, keep3, w)
    dnorm3 = norm_terms(dqkv3, w)
    x2c = chunk(h2).astype(F32)
    inv3c, _ = norm_chunk(x2c, gain)
    g2c = chunk(g3).astype(F32) + norm_grad(sum_chunk(dnorm3), x2c, inv3c, gain)
    g2 = all_rows(g2c.astype(BF))

    dqkv2 = backward(g2, keep2, w)

    def product(left3, right3, left2, right2):
        both = dot(jnp.concatenate([left3, left2], 0), jnp.concatenate([right3, right2], 0), tokens)
        return both.astype(BF).reshape(NP, NN, 32, HD)

    terms = [product(rows3, d3, rows2, d2) for d3, d2 in zip(dqkv3, dqkv2)]
    terms.append(product(dy3, keep3[-1], g2, attn2))
    terms = jnp.stack(terms, 2).transpose(1, 0, 2, 3, 4)
    terms = with_layout_constraint(terms, Layout((0, 1, 2, 3, 4)))
    terms, dqkv2, old_h, old_g = lax.optimization_barrier((terms, dqkv2, h2, g2))
    terms = swap(terms, NEAR)
    base_h = jnp.where(mine, old_h, hidden_in[0])
    base_g = jnp.where(mine, old_g, cotangent[0])
    dnorm2 = norm_terms(dqkv2, w)

    mixed3 = mixed3.astype(BF)
    tile = add(jnp.where(core == 0, mixed3, dnorm2), from_core(jnp.where(core == 0, dnorm2, mixed3)))
    tile = add(tile, from_pair(tile, 1))
    pair = from_pair(tile, 3)

    part = sum_terms(terms)
    shards = swap(part, "zp")

    tile, pair, _ = lax.optimization_barrier((tile, pair, part))
    tile = add(tile, pair)
    other = from_core(tile)
    flags = jnp.stack([core, mine.astype(jnp.int32)])
    hidden_out, grad_in = last_step(flags, tile, other, base_h, base_g, h1, inv2, gain)
    shards, hidden_out, grad_in = lax.optimization_barrier((shards, hidden_out, grad_in))
    shard = jnp.sum(shards.astype(F32), 0)
    return (hidden_out[None], grad_in[None], shard[:3], shard[3].T)


def solution(mesh):
    grid = Mesh(mesh.devices.reshape(NP, 2, NN // 2, CTX // 2, 2), ("zp", "zq", "y") + CONTEXT)
    dp = ("zp", "zq", "y")
    in_specs = (
        P(dp, CONTEXT, None),
        P(dp, CONTEXT, None),
        P(dp, None),
        P(None, dp, CONTEXT),
        P(CONTEXT, dp),
        P(),
    )
    out_specs = (
        P(dp, CONTEXT, None),
        P(dp, CONTEXT, None),
        P(None, dp, CONTEXT),
        P(CONTEXT, dp),
    )
    return jax.shard_map(
        on_device, mesh=grid, in_specs=in_specs, out_specs=out_specs, check_vma=False
    )
```

```python
import jax
import jax.numpy as jnp
from jax import lax
from jax.experimental import pallas as pl
from jax.experimental.pallas import tpu as pltpu
from jax.sharding import Mesh, PartitionSpec as P

HD = 128
TILE = 128
D = 2048
CTX = 8
NP = 8
NN = 8
NEAR = ("zq", "y")
CHUNK = TILE // CTX
SCALE = HD**-0.5
CONTEXT = ("x", "core")
BF = jnp.bfloat16
F32 = jnp.float32


def swap(x, axis):
    return lax.all_to_all(x, axis, 0, 0)


def spread(x, axis, size):
    return swap(jnp.broadcast_to(x[None], (size,) + x.shape), axis)


def dot(a, b, dims):
    return lax.dot_general(a, b, (dims, ((), ())), preferred_element_type=F32)


def add(a, b):
    return (a.astype(F32) + b.astype(F32)).astype(BF)


def from_core(x):
    return lax.ppermute(x, "core", [(0, 1), (1, 0)])


def from_pair(x, bit):
    return lax.ppermute(x, "x", [(i, i ^ bit) for i in range(CTX // 2)])


def norm_chunk(x32, gain):
    inv = lax.rsqrt(jnp.mean(x32 * x32, -1, keepdims=True) + 1e-06)
    return inv, (x32 * inv * gain).astype(BF)


def all_rows(chunk):
    return lax.all_gather(chunk, CONTEXT, tiled=True)


def sum_chunk(terms):
    return jnp.sum(swap(terms.astype(BF).reshape(CTX, CHUNK, D), CONTEXT).astype(F32), 0)


def forward(rows, w):
    q = dot(rows, w[0], ((1,), (0,))).astype(BF)
    k = dot(rows, w[1], ((1,), (0,))).astype(BF)
    v = dot(rows, w[2], ((1,), (0,))).astype(BF)
    pos = jnp.arange(TILE)
    scores = dot(q, k, ((1,), (1,))) * SCALE
    scores = jnp.where(pos[None, :] <= pos[:, None], scores, -1e30)
    expo = jnp.exp(scores - jnp.max(scores, -1, keepdims=True))
    prob = expo / jnp.sum(expo, -1, keepdims=True)
    probb = prob.astype(BF)
    attn = dot(probb, v, ((1,), (0,))).astype(BF)
    mixed = dot(attn, w[3], ((1,), (1,)))
    return mixed, (rows, q, k, v, prob, probb, attn)


def backward(dy, keep, w):
    rows, q, k, v, prob, probb, attn = keep
    dattn = dot(dy, w[3], ((1,), (0,))).astype(BF)
    delta = jnp.sum(dattn.astype(F32) * attn.astype(F32), -1, keepdims=True)
    dprob = dot(dattn, v, ((1,), (1,)))
    dscore = (prob * (dprob - delta) * SCALE).astype(BF)
    dq = dot(dscore, k, ((1,), (0,))).astype(BF)
    dk = dot(dscore, q, ((0,), (0,))).astype(BF)
    dv = dot(probb, dattn, ((0,), (0,))).astype(BF)
    return dq, dk, dv


def norm_terms(dqkv, w):
    dq, dk, dv = dqkv
    total = dot(dq, w[0], ((1,), (1,))) + dot(dk, w[1], ((1,), (1,))) + dot(dv, w[2], ((1,), (1,)))
    return total.astype(BF)


def norm_grad(e, x32, inv, gain):
    u = e * gain
    return inv * u - x32 * inv**3 * jnp.mean(x32 * u, -1, keepdims=True)


def first_kernel(depth, h, g, w_qkv, w_out, sent, shards, qkv_in, out_in, sems):
    core = lax.axis_index("core")
    live = depth[0, lax.axis_index("x") * 2 + core] >= 2
    weights = [
        pltpu.make_async_copy(w_qkv, qkv_in, sems.at[0]),
        pltpu.make_async_copy(w_out, out_in, sems.at[1]),
    ]
    for copy in weights:
        copy.start()

    @pl.when(live & (core == 0))
    def _():
        copy = pltpu.make_async_copy(g, sent, sems.at[2])
        copy.start()
        copy.wait()

    @pl.when(live & (core == 1))
    def _():
        copy = pltpu.make_async_copy(h, sent, sems.at[3])
        copy.start()
        copy.wait()

    @pl.when(jnp.logical_not(live))
    def _():
        sent[...] = jnp.zeros_like(sent)

    for copy in weights:
        copy.wait()
    for i in range(NP):
        shards[i, :3] = qkv_in[...]
        shards[i, 3] = out_in[...]


def first_step(depth, h, g, w_qkv, w_out):
    return pl.pallas_call(
        first_kernel,
        in_specs=[pl.BlockSpec(memory_space=pltpu.SMEM)] + [pl.BlockSpec(memory_space=pl.ANY)] * 4,
        out_specs=[pl.BlockSpec(memory_space=pltpu.VMEM)] * 2,
        out_shape=[
            jax.ShapeDtypeStruct((TILE, D), BF),
            jax.ShapeDtypeStruct((NP, 4, 32, HD), BF),
        ],
        scratch_shapes=[
            pltpu.VMEM((3, 32, HD), BF),
            pltpu.VMEM((32, HD), BF),
            pltpu.SemaphoreType.DMA((4,)),
        ],
        compiler_params=pltpu.CompilerParams(vmem_limit_bytes=60 * 2**20),
    )(depth, h, g, w_qkv, w_out)


def products_kernel(rows_t, dqkv3, dq, dk, dv, out, terms, both, block, sems):
    both[:TILE] = dqkv3[...]
    for t, part in enumerate((dq, dk, dv)):
        both[TILE:, t * HD : (t + 1) * HD] = part[...]
    size = D // NP
    parts = []
    for p in range(NP):
        grad = dot(rows_t[p * size : (p + 1) * size, :], both[...], ((1,), (0,))).astype(BF)
        for n in range(NN):
            rows = slice(n * 32, (n + 1) * 32)
            for t in range(3):
                block[p, n, t] = grad[rows, t * HD : (t + 1) * HD]
            block[p, n, 3] = out[p * size + n * 32 : p * size + (n + 1) * 32, :]
        parts.append(pltpu.make_async_copy(block.at[p], terms.at[:, p], sems.at[p]))
        parts[-1].start()
    for part in parts:
        part.wait()


def products(rows_t, dqkv3, dqkv2, out):
    return pl.pallas_call(
        products_kernel,
        in_specs=[pl.BlockSpec(memory_space=pltpu.VMEM)] * 6,
        out_specs=pl.BlockSpec(memory_space=pl.ANY),
        out_shape=jax.ShapeDtypeStruct((NN, NP, 4, 32, HD), BF),
        scratch_shapes=[
            pltpu.VMEM((2 * TILE, 3 * HD), BF),
            pltpu.VMEM((NP, NN, 4, 32, HD), BF),
            pltpu.SemaphoreType.DMA((NP,)),
        ],
        compiler_params=pltpu.CompilerParams(vmem_limit_bytes=60 * 2**20),
    )(rows_t, dqkv3, *dqkv2, out)


def sum_kernel(terms, out):
    total = terms[0].astype(F32)
    for i in range(1, NN):
        total = total + terms[i].astype(F32)
    out[...] = total.astype(BF)


def sum_terms(terms):
    return pl.pallas_call(
        sum_kernel,
        grid=(NP // 2,),
        in_specs=[pl.BlockSpec((NN, 2, 4, 32, HD), lambda i: (0, i, 0, 0, 0))],
        out_specs=pl.BlockSpec((2, 4, 32, HD), lambda i: (i, 0, 0, 0)),
        out_shape=jax.ShapeDtypeStruct((NP, 4, 32, HD), BF),
        compiler_params=pltpu.CompilerParams(vmem_limit_bytes=16 * 2**20),
    )(terms)


def last_kernel(flags, tile, other, base_h, base_g, h1, inv, gain, out_h, out_g):
    first, mine = flags[0] == 0, flags[1] == 1
    a, b = tile[...].astype(F32), other[...].astype(F32)
    old_h, old_g = base_h[...], base_g[...]
    new_h = (old_h.astype(F32) + jnp.where(first, a, b)).astype(BF)
    dx = norm_grad(jnp.where(first, b, a), h1[...].astype(F32), inv[...], gain[...])
    new_g = (old_g.astype(F32) + dx).astype(BF)
    out_h[...] = jnp.where(mine, new_h, old_h)
    out_g[...] = jnp.where(mine, new_g, old_g)


def last_step(flags, tile, other, base_h, base_g, h1, inv, gain):
    steps = 4
    rows = pl.BlockSpec((TILE // steps, D), lambda i: (i, 0))
    return pl.pallas_call(
        last_kernel,
        grid=(steps,),
        in_specs=[pl.BlockSpec(memory_space=pltpu.SMEM)]
        + [rows] * 5
        + [pl.BlockSpec((TILE // steps, 1), lambda i: (i, 0)), pl.BlockSpec((1, D), lambda i: (0, 0))],
        out_specs=[rows, rows],
        out_shape=[jax.ShapeDtypeStruct((TILE, D), BF)] * 2,
        compiler_params=pltpu.CompilerParams(vmem_limit_bytes=16 * 2**20),
    )(flags, tile, other, base_h, base_g, h1, inv, gain.reshape(1, D))


def on_device(hidden_in, cotangent, tile_depth, w_qkv, w_out, gain):
    me = lax.axis_index("x") * 2 + lax.axis_index("core")
    depth = tile_depth[0]
    live3 = jnp.any(depth >= 3)
    mine = lax.dynamic_index_in_dim(depth, me, 0, keepdims=False) >= 2

    def chunk(tile):
        return lax.dynamic_index_in_dim(tile.reshape(CTX, CHUNK, D), me, 0, keepdims=False)

    tokens = ((0,), (0,))
    core = lax.axis_index("core")
    none = jnp.zeros_like(hidden_in[0])
    sent, shards = first_step(tile_depth, hidden_in[0], cotangent[0], w_qkv, w_out.T)
    kept = jnp.where(mine, jnp.where(core == 0, hidden_in[0], cotangent[0]), none)
    tile = kept + from_core(sent)
    tile = tile + from_pair(tile, 1)

    near = swap(shards, "zp")
    near, tile = lax.optimization_barrier((near, tile))
    w = spread(near, NEAR, NN).transpose(2, 1, 0, 3, 4).reshape(4, D, HD)
    tile = tile + from_pair(tile, 3)
    other = from_core(tile)
    h1, g3 = jnp.where(core == 0, tile, other), jnp.where(core == 0, other, tile)

    x1 = h1.astype(F32)
    inv2, rows2 = norm_chunk(x1, gain)
    mixed2, keep2 = forward(rows2, w)
    attn2 = keep2[-1]
    h2c = (chunk(h1).astype(F32) + sum_chunk(mixed2)).astype(BF)
    h2 = all_rows(h2c)

    x2 = h2.astype(F32)
    inv3, normed3 = norm_chunk(x2, gain)
    rows3 = jnp.where(live3, normed3, jnp.zeros_like(normed3))
    dy3 = jnp.where(live3, g3, jnp.zeros_like(g3))
    rows3 = lax.optimization_barrier(rows3)
    mixed3, keep3 = forward(rows3, w)
    dqkv3 = backward(dy3, keep3, w)
    dnorm3 = norm_terms(dqkv3, w)
    x2c = chunk(h2).astype(F32)
    inv3c, _ = norm_chunk(x2c, gain)
    g2c = chunk(g3).astype(F32) + norm_grad(sum_chunk(dnorm3), x2c, inv3c, gain)
    g2 = all_rows(g2c.astype(BF))

    dqkv2 = backward(g2, keep2, w)

    out = jnp.concatenate([dy3, g2], 0), jnp.concatenate([keep3[-1], attn2], 0)
    out = dot(out[0], out[1], tokens).astype(BF)
    rows_t = jnp.concatenate([rows3, rows2], 0).T
    terms = products(rows_t, jnp.concatenate(dqkv3, 1), dqkv2, out)
    terms, dqkv2, old_h, old_g = lax.optimization_barrier((terms, dqkv2, h2, g2))
    terms = swap(terms, NEAR)
    base_h = jnp.where(mine, old_h, hidden_in[0])
    base_g = jnp.where(mine, old_g, cotangent[0])
    dnorm2 = norm_terms(dqkv2, w)

    mixed3 = mixed3.astype(BF)
    tile = add(jnp.where(core == 0, mixed3, dnorm2), from_core(jnp.where(core == 0, dnorm2, mixed3)))
    tile = add(tile, from_pair(tile, 1))
    pair = from_pair(tile, 3)

    part = sum_terms(terms)
    shards = swap(part, "zp")

    tile, pair, _ = lax.optimization_barrier((tile, pair, part))
    tile = add(tile, pair)
    other = from_core(tile)
    flags = jnp.stack([core, mine.astype(jnp.int32)])
    hidden_out, grad_in = last_step(flags, tile, other, base_h, base_g, h1, inv2, gain)
    shards, hidden_out, grad_in = lax.optimization_barrier((shards, hidden_out, grad_in))
    shard = jnp.sum(shards.astype(F32), 0)
    return (hidden_out[None], grad_in[None], shard[:3], shard[3].T)


def solution(mesh):
    grid = Mesh(mesh.devices.reshape(NP, 2, NN // 2, CTX // 2, 2), ("zp", "zq", "y") + CONTEXT)
    dp = ("zp", "zq", "y")
    in_specs = (
        P(dp, CONTEXT, None),
        P(dp, CONTEXT, None),
        P(dp, None),
        P(None, dp, CONTEXT),
        P(CONTEXT, dp),
        P(),
    )
    out_specs = (
        P(dp, CONTEXT, None),
        P(dp, CONTEXT, None),
        P(None, dp, CONTEXT),
        P(CONTEXT, dp),
    )
    return jax.shard_map(
        on_device, mesh=grid, in_specs=in_specs, out_specs=out_specs, check_vma=False
    )
```

```python
import jax
import jax.numpy as jnp
from jax import lax
from jax.experimental import pallas as pl
from jax.experimental.layout import Layout, with_layout_constraint
from jax.experimental.pallas import tpu as pltpu
from jax.sharding import Mesh, PartitionSpec as P

HD = 128
TILE = 128
D = 2048
CTX = 8
NP = 8
NN = 8
NEAR = ("zq", "y")
CHUNK = TILE // CTX
SCALE = HD**-0.5
CONTEXT = ("x", "core")
BF = jnp.bfloat16
F32 = jnp.float32


def swap(x, axis):
    return lax.all_to_all(x, axis, 0, 0)


def spread(x, axis, size):
    return swap(jnp.broadcast_to(x[None], (size,) + x.shape), axis)


def dot(a, b, dims):
    return lax.dot_general(a, b, (dims, ((), ())), preferred_element_type=F32)


def add(a, b):
    return (a.astype(F32) + b.astype(F32)).astype(BF)


def from_core(x):
    return lax.ppermute(x, "core", [(0, 1), (1, 0)])


def from_pair(x, bit):
    return lax.ppermute(x, "x", [(i, i ^ bit) for i in range(CTX // 2)])


def norm_chunk(x32, gain):
    inv = lax.rsqrt(jnp.mean(x32 * x32, -1, keepdims=True) + 1e-06)
    return inv, (x32 * inv * gain).astype(BF)


def all_rows(chunk):
    return lax.all_gather(chunk, CONTEXT, tiled=True)


def sum_chunk(terms):
    return jnp.sum(swap(terms.astype(BF).reshape(CTX, CHUNK, D), CONTEXT).astype(F32), 0)


def forward(rows, w):
    q = dot(rows, w[0], ((1,), (0,))).astype(BF)
    k = dot(rows, w[1], ((1,), (0,))).astype(BF)
    v = dot(rows, w[2], ((1,), (0,))).astype(BF)
    pos = jnp.arange(TILE)
    scores = dot(q, k, ((1,), (1,))) * SCALE
    scores = jnp.where(pos[None, :] <= pos[:, None], scores, -1e30)
    expo = jnp.exp(scores - jnp.max(scores, -1, keepdims=True))
    prob = expo / jnp.sum(expo, -1, keepdims=True)
    probb = prob.astype(BF)
    attn = dot(probb, v, ((1,), (0,))).astype(BF)
    mixed = dot(attn, w[3], ((1,), (1,)))
    return mixed, (rows, q, k, v, prob, probb, attn)


def backward(dy, keep, w):
    rows, q, k, v, prob, probb, attn = keep
    dattn = dot(dy, w[3], ((1,), (0,))).astype(BF)
    delta = jnp.sum(dattn.astype(F32) * attn.astype(F32), -1, keepdims=True)
    dprob = dot(dattn, v, ((1,), (1,)))
    dscore = (prob * (dprob - delta) * SCALE).astype(BF)
    dq = dot(dscore, k, ((1,), (0,))).astype(BF)
    dk = dot(dscore, q, ((0,), (0,))).astype(BF)
    dv = dot(probb, dattn, ((0,), (0,))).astype(BF)
    return dq, dk, dv


def norm_terms(dqkv, w):
    dq, dk, dv = dqkv
    total = dot(dq, w[0], ((1,), (1,))) + dot(dk, w[1], ((1,), (1,))) + dot(dv, w[2], ((1,), (1,)))
    return total.astype(BF)


def norm_grad(e, x32, inv, gain):
    u = e * gain
    return inv * u - x32 * inv**3 * jnp.mean(x32 * u, -1, keepdims=True)


def first_kernel(depth, h, g, w_qkv, w_out, sent, shards, qkv_in, out_in, sems):
    core = lax.axis_index("core")
    live = depth[0, lax.axis_index("x") * 2 + core] >= 2
    weights = [
        pltpu.make_async_copy(w_qkv, qkv_in, sems.at[0]),
        pltpu.make_async_copy(w_out, out_in, sems.at[1]),
    ]
    for copy in weights:
        copy.start()

    @pl.when(live & (core == 0))
    def _():
        copy = pltpu.make_async_copy(g, sent, sems.at[2])
        copy.start()
        copy.wait()

    @pl.when(live & (core == 1))
    def _():
        copy = pltpu.make_async_copy(h, sent, sems.at[3])
        copy.start()
        copy.wait()

    @pl.when(jnp.logical_not(live))
    def _():
        sent[...] = jnp.zeros_like(sent)

    for copy in weights:
        copy.wait()
    for i in range(NP):
        shards[i, :3] = qkv_in[...]
        shards[i, 3] = out_in[...]


def first_step(depth, h, g, w_qkv, w_out):
    return pl.pallas_call(
        first_kernel,
        in_specs=[pl.BlockSpec(memory_space=pltpu.SMEM)] + [pl.BlockSpec(memory_space=pl.ANY)] * 4,
        out_specs=[pl.BlockSpec(memory_space=pltpu.VMEM)] * 2,
        out_shape=[
            jax.ShapeDtypeStruct((TILE, D), BF),
            jax.ShapeDtypeStruct((NP, 4, 32, HD), BF),
        ],
        scratch_shapes=[
            pltpu.VMEM((3, 32, HD), BF),
            pltpu.VMEM((32, HD), BF),
            pltpu.SemaphoreType.DMA((4,)),
        ],
        compiler_params=pltpu.CompilerParams(vmem_limit_bytes=60 * 2**20),
    )(depth, h, g, w_qkv, w_out)


def sum_kernel(terms, out):
    total = terms[0].astype(F32)
    for i in range(1, NN):
        total = total + terms[i].astype(F32)
    out[...] = total.astype(BF)


def sum_terms(terms):
    return pl.pallas_call(
        sum_kernel,
        grid=(NP // 2,),
        in_specs=[pl.BlockSpec((NN, 2, 4, 32, HD), lambda i: (0, i, 0, 0, 0))],
        out_specs=pl.BlockSpec((2, 4, 32, HD), lambda i: (i, 0, 0, 0)),
        out_shape=jax.ShapeDtypeStruct((NP, 4, 32, HD), BF),
        compiler_params=pltpu.CompilerParams(vmem_limit_bytes=16 * 2**20),
    )(terms)


def last_kernel(flags, tile, other, base_h, base_g, h1, inv, gain, out_h, out_g):
    first, mine = flags[0] == 0, flags[1] == 1
    a, b = tile[...].astype(F32), other[...].astype(F32)
    old_h, old_g = base_h[...], base_g[...]
    new_h = (old_h.astype(F32) + jnp.where(first, a, b)).astype(BF)
    dx = norm_grad(jnp.where(first, b, a), h1[...].astype(F32), inv[...], gain[...])
    new_g = (old_g.astype(F32) + dx).astype(BF)
    out_h[...] = jnp.where(mine, new_h, old_h)
    out_g[...] = jnp.where(mine, new_g, old_g)


def last_step(flags, tile, other, base_h, base_g, h1, inv, gain):
    steps = 4
    rows = pl.BlockSpec((TILE // steps, D), lambda i: (i, 0))
    return pl.pallas_call(
        last_kernel,
        grid=(steps,),
        in_specs=[pl.BlockSpec(memory_space=pltpu.SMEM)]
        + [rows] * 5
        + [pl.BlockSpec((TILE // steps, 1), lambda i: (i, 0)), pl.BlockSpec((1, D), lambda i: (0, 0))],
        out_specs=[rows, rows],
        out_shape=[jax.ShapeDtypeStruct((TILE, D), BF)] * 2,
        compiler_params=pltpu.CompilerParams(vmem_limit_bytes=16 * 2**20),
    )(flags, tile, other, base_h, base_g, h1, inv, gain.reshape(1, D))


def on_device(hidden_in, cotangent, tile_depth, w_qkv, w_out, gain):
    me = lax.axis_index("x") * 2 + lax.axis_index("core")
    depth = tile_depth[0]
    live3 = jnp.any(depth >= 3)
    mine = lax.dynamic_index_in_dim(depth, me, 0, keepdims=False) >= 2

    def chunk(tile):
        return lax.dynamic_index_in_dim(tile.reshape(CTX, CHUNK, D), me, 0, keepdims=False)

    tokens = ((0,), (0,))
    core = lax.axis_index("core")
    none = jnp.zeros_like(hidden_in[0])
    sent, shards = first_step(tile_depth, hidden_in[0], cotangent[0], w_qkv, w_out.T)
    kept = jnp.where(mine, jnp.where(core == 0, hidden_in[0], cotangent[0]), none)
    tile = kept + from_core(sent)
    tile = tile + from_pair(tile, 1)

    near = swap(shards, "zp")
    near, tile = lax.optimization_barrier((near, tile))
    w = spread(near, NEAR, NN).transpose(2, 1, 0, 3, 4).reshape(4, D, HD)
    tile = tile + from_pair(tile, 3)
    other = from_core(tile)
    h1, g3 = jnp.where(core == 0, tile, other), jnp.where(core == 0, other, tile)
    dy3 = jnp.where(live3, g3, jnp.zeros_like(g3))
    h1, g3, dy3 = lax.optimization_barrier((h1, g3, dy3))

    x1 = h1.astype(F32)
    inv2, rows2 = norm_chunk(x1, gain)
    mixed2, keep2 = forward(rows2, w)
    attn2 = keep2[-1]
    h2c = (chunk(h1).astype(F32) + sum_chunk(mixed2)).astype(BF)
    h2 = all_rows(h2c)

    h2, dy3 = lax.optimization_barrier((h2, dy3))
    x2 = h2.astype(F32)
    inv3, normed3 = norm_chunk(x2, gain)
    rows3 = jnp.where(live3, normed3, jnp.zeros_like(normed3))
    rows3 = lax.optimization_barrier(rows3)
    mixed3, keep3 = forward(rows3, w)
    dqkv3 = backward(dy3, keep3, w)
    dnorm3 = norm_terms(dqkv3, w)
    x2c = chunk(h2).astype(F32)
    inv3c, _ = norm_chunk(x2c, gain)
    g2c = chunk(g3).astype(F32) + norm_grad(sum_chunk(dnorm3), x2c, inv3c, gain)
    g2 = all_rows(g2c.astype(BF))

    dqkv2 = backward(g2, keep2, w)

    def product(left3, right3, left2, right2):
        both = dot(jnp.concatenate([left3, left2], 0), jnp.concatenate([right3, right2], 0), tokens)
        return both.astype(BF).reshape(NP, NN, 32, HD)

    terms = [product(rows3, d3, rows2, d2) for d3, d2 in zip(dqkv3, dqkv2)]
    terms.append(product(dy3, keep3[-1], g2, attn2))
    terms = jnp.stack(terms, 2).transpose(1, 0, 2, 3, 4)
    terms = with_layout_constraint(terms, Layout((0, 1, 2, 3, 4)))
    terms, dqkv2, old_h, old_g = lax.optimization_barrier((terms, dqkv2, h2, g2))
    terms = swap(terms, NEAR)
    base_h = jnp.where(mine, old_h, hidden_in[0])
    base_g = jnp.where(mine, old_g, cotangent[0])
    dnorm2 = norm_terms(dqkv2, w)

    mixed3 = mixed3.astype(BF)
    tile = add(jnp.where(core == 0, mixed3, dnorm2), from_core(jnp.where(core == 0, dnorm2, mixed3)))
    tile = add(tile, from_pair(tile, 1))
    pair = from_pair(tile, 3)

    part = sum_terms(terms)
    shards = swap(part, "zp")

    tile, pair, _ = lax.optimization_barrier((tile, pair, part))
    tile = add(tile, pair)
    other = from_core(tile)
    flags = jnp.stack([core, mine.astype(jnp.int32)])
    hidden_out, grad_in = last_step(flags, tile, other, base_h, base_g, h1, inv2, gain)
    shards, hidden_out, grad_in = lax.optimization_barrier((shards, hidden_out, grad_in))
    grad_qkv = jnp.sum(shards[:, :3].astype(F32), 0)
    grad_out = jnp.sum(shards[:, 3].astype(F32), 0).T
    return (hidden_out[None], grad_in[None], grad_qkv, grad_out)


def solution(mesh):
    grid = Mesh(mesh.devices.reshape(NP, 2, NN // 2, CTX // 2, 2), ("zp", "zq", "y") + CONTEXT)
    dp = ("zp", "zq", "y")
    in_specs = (
        P(dp, CONTEXT, None),
        P(dp, CONTEXT, None),
        P(dp, None),
        P(None, dp, CONTEXT),
        P(CONTEXT, dp),
        P(),
    )
    out_specs = (
        P(dp, CONTEXT, None),
        P(dp, CONTEXT, None),
        P(None, dp, CONTEXT),
        P(CONTEXT, dp),
    )
    return jax.shard_map(
        on_device, mesh=grid, in_specs=in_specs, out_specs=out_specs, check_vma=False
    )
```

```python
import jax
import jax.numpy as jnp
from jax import lax
from jax.experimental import pallas as pl
from jax.experimental.layout import Layout, with_layout_constraint
from jax.experimental.pallas import tpu as pltpu
from jax.sharding import Mesh, PartitionSpec as P

HD = 128
TILE = 128
D = 2048
CTX = 8
NP = 8
NN = 8
NEAR = ("zq", "y")
CHUNK = TILE // CTX
SCALE = HD**-0.5
CONTEXT = ("x", "core")
BF = jnp.bfloat16
F32 = jnp.float32


def swap(x, axis):
    return lax.all_to_all(x, axis, 0, 0)


def spread(x, axis, size):
    return swap(jnp.broadcast_to(x[None], (size,) + x.shape), axis)


def dot(a, b, dims):
    return lax.dot_general(a, b, (dims, ((), ())), preferred_element_type=F32)


def add(a, b):
    return (a.astype(F32) + b.astype(F32)).astype(BF)


def from_core(x):
    return lax.ppermute(x, "core", [(0, 1), (1, 0)])


def from_pair(x, bit):
    return lax.ppermute(x, "x", [(i, i ^ bit) for i in range(CTX // 2)])


def norm_chunk(x32, gain):
    inv = lax.rsqrt(jnp.mean(x32 * x32, -1, keepdims=True) + 1e-06)
    return inv, (x32 * inv * gain).astype(BF)


def all_rows(chunk):
    return lax.all_gather(chunk, CONTEXT, tiled=True)


def sum_chunk(terms):
    return jnp.sum(swap(terms.astype(BF).reshape(CTX, CHUNK, D), CONTEXT).astype(F32), 0)


def forward(rows, w):
    q = dot(rows, w[0], ((1,), (0,))).astype(BF)
    k = dot(rows, w[1], ((1,), (0,))).astype(BF)
    v = dot(rows, w[2], ((1,), (0,))).astype(BF)
    pos = jnp.arange(TILE)
    scores = dot(q, k, ((1,), (1,))) * SCALE
    scores = jnp.where(pos[None, :] <= pos[:, None], scores, -1e30)
    expo = jnp.exp(scores - jnp.max(scores, -1, keepdims=True))
    prob = expo / jnp.sum(expo, -1, keepdims=True)
    probb = prob.astype(BF)
    attn = dot(probb, v, ((1,), (0,))).astype(BF)
    mixed = dot(attn, w[3], ((1,), (1,)))
    return mixed, (rows, q, k, v, prob, probb, attn)


def backward(dy, keep, w):
    rows, q, k, v, prob, probb, attn = keep
    dattn = dot(dy, w[3], ((1,), (0,))).astype(BF)
    delta = jnp.sum(dattn.astype(F32) * attn.astype(F32), -1, keepdims=True)
    dprob = dot(dattn, v, ((1,), (1,)))
    dscore = (prob * (dprob - delta) * SCALE).astype(BF)
    dq = dot(dscore, k, ((1,), (0,))).astype(BF)
    dk = dot(dscore, q, ((0,), (0,))).astype(BF)
    dv = dot(probb, dattn, ((0,), (0,))).astype(BF)
    return dq, dk, dv


def norm_terms(dqkv, w):
    dq, dk, dv = dqkv
    total = dot(dq, w[0], ((1,), (1,))) + dot(dk, w[1], ((1,), (1,))) + dot(dv, w[2], ((1,), (1,)))
    return total.astype(BF)


def norm_grad(e, x32, inv, gain):
    u = e * gain
    return inv * u - x32 * inv**3 * jnp.mean(x32 * u, -1, keepdims=True)


def first_kernel(h, g, w_qkv, w_out, sent, shards, sems, tile_sems):
    parts = []
    for i in range(NP):
        parts.append(pltpu.make_async_copy(w_qkv, shards.at[i, pl.ds(0, 3)], sems.at[i, 0]))
        parts.append(pltpu.make_async_copy(w_out, shards.at[i, 3], sems.at[i, 1]))
    for part in parts:
        part.start()
    core = lax.axis_index("core")
    for i, tile in enumerate((g, h)):

        @pl.when(core == i)
        def _(i=i, tile=tile):
            copy = pltpu.make_async_copy(tile, sent, tile_sems.at[i])
            copy.start()
            copy.wait()

    for part in parts:
        part.wait()


def first_step(h, g, w_qkv, w_out):
    return pl.pallas_call(
        first_kernel,
        in_specs=[pl.BlockSpec(memory_space=pl.ANY)] * 4,
        out_specs=[pl.BlockSpec(memory_space=pl.ANY)] * 2,
        out_shape=[
            jax.ShapeDtypeStruct((TILE, D), BF),
            jax.ShapeDtypeStruct((NP, 4, 32, HD), BF),
        ],
        scratch_shapes=[pltpu.SemaphoreType.DMA((NP, 2)), pltpu.SemaphoreType.DMA((2,))],
        compiler_params=pltpu.CompilerParams(vmem_limit_bytes=60 * 2**20),
    )(h, g, w_qkv, w_out)


def sum_kernel(terms, out):
    total = terms[0].astype(F32)
    for i in range(1, NN):
        total = total + terms[i].astype(F32)
    out[...] = total.astype(BF)


def sum_terms(terms):
    return pl.pallas_call(
        sum_kernel,
        grid=(NP // 2,),
        in_specs=[pl.BlockSpec((NN, 2, 4, 32, HD), lambda i: (0, i, 0, 0, 0))],
        out_specs=pl.BlockSpec((2, 4, 32, HD), lambda i: (i, 0, 0, 0)),
        out_shape=jax.ShapeDtypeStruct((NP, 4, 32, HD), BF),
        compiler_params=pltpu.CompilerParams(vmem_limit_bytes=16 * 2**20),
    )(terms)


def last_kernel(flags, tile, other, base_h, base_g, h1, inv, gain, out_h, out_g):
    first, mine = flags[0] == 0, flags[1] == 1
    a, b = tile[...].astype(F32), other[...].astype(F32)
    old_h, old_g = base_h[...], base_g[...]
    new_h = (old_h.astype(F32) + jnp.where(first, a, b)).astype(BF)
    dx = norm_grad(jnp.where(first, b, a), h1[...].astype(F32), inv[...], gain[...])
    new_g = (old_g.astype(F32) + dx).astype(BF)
    out_h[...] = jnp.where(mine, new_h, old_h)
    out_g[...] = jnp.where(mine, new_g, old_g)


def last_step(flags, tile, other, base_h, base_g, h1, inv, gain):
    steps = 4
    rows = pl.BlockSpec((TILE // steps, D), lambda i: (i, 0))
    return pl.pallas_call(
        last_kernel,
        grid=(steps,),
        in_specs=[pl.BlockSpec(memory_space=pltpu.SMEM)]
        + [rows] * 5
        + [pl.BlockSpec((TILE // steps, 1), lambda i: (i, 0)), pl.BlockSpec((1, D), lambda i: (0, 0))],
        out_specs=[rows, rows],
        out_shape=[jax.ShapeDtypeStruct((TILE, D), BF)] * 2,
        compiler_params=pltpu.CompilerParams(vmem_limit_bytes=16 * 2**20),
    )(flags, tile, other, base_h, base_g, h1, inv, gain.reshape(1, D))


def on_device(hidden_in, cotangent, tile_depth, w_qkv, w_out, gain):
    me = lax.axis_index("x") * 2 + lax.axis_index("core")
    depth = tile_depth[0]
    live3 = jnp.any(depth >= 3)
    mine = lax.dynamic_index_in_dim(depth, me, 0, keepdims=False) >= 2

    def chunk(tile):
        return lax.dynamic_index_in_dim(tile.reshape(CTX, CHUNK, D), me, 0, keepdims=False)

    tokens = ((0,), (0,))
    core = lax.axis_index("core")
    none = jnp.zeros_like(hidden_in[0])
    sent, shards = first_step(hidden_in[0], cotangent[0], w_qkv, w_out.T)
    near_mine = lax.dynamic_index_in_dim(depth, me + 1 - 2 * core, 0, keepdims=False) >= 2
    kept = jnp.where(mine, jnp.where(core == 0, hidden_in[0], cotangent[0]), none)
    tile = jnp.where(near_mine, from_core(sent), kept)
    tile = tile + from_pair(tile, 1)

    near = swap(shards, "zp")
    near, tile = lax.optimization_barrier((near, tile))
    w = spread(near, NEAR, NN).transpose(2, 1, 0, 3, 4).reshape(4, D, HD)
    tile = tile + from_pair(tile, 3)
    other = from_core(tile)
    h1, g3 = jnp.where(core == 0, tile, other), jnp.where(core == 0, other, tile)
    dy3 = jnp.where(live3, g3, jnp.zeros_like(g3))
    h1, g3, dy3 = lax.optimization_barrier((h1, g3, dy3))

    x1 = h1.astype(F32)
    inv2, rows2 = norm_chunk(x1, gain)
    mixed2, keep2 = forward(rows2, w)
    attn2 = keep2[-1]
    h2c = (chunk(h1).astype(F32) + sum_chunk(mixed2)).astype(BF)
    h2 = all_rows(h2c)

    h2, dy3 = lax.optimization_barrier((h2, dy3))
    x2 = h2.astype(F32)
    inv3, normed3 = norm_chunk(x2, gain)
    rows3 = jnp.where(live3, normed3, jnp.zeros_like(normed3))
    rows3 = lax.optimization_barrier(rows3)
    mixed3, keep3 = forward(rows3, w)
    dqkv3 = backward(dy3, keep3, w)
    dnorm3 = norm_terms(dqkv3, w)
    x2c = chunk(h2).astype(F32)
    inv3c, _ = norm_chunk(x2c, gain)
    g2c = chunk(g3).astype(F32) + norm_grad(sum_chunk(dnorm3), x2c, inv3c, gain)
    g2 = all_rows(g2c.astype(BF))

    dqkv2 = backward(g2, keep2, w)

    def product(left3, right3, left2, right2):
        both = dot(jnp.concatenate([left3, left2], 0), jnp.concatenate([right3, right2], 0), tokens)
        return both.astype(BF).reshape(NP, NN, 32, HD)

    terms = [product(rows3, d3, rows2, d2) for d3, d2 in zip(dqkv3, dqkv2)]
    terms.append(product(dy3, keep3[-1], g2, attn2))
    terms = jnp.stack(terms, 2).transpose(1, 0, 2, 3, 4)
    terms = with_layout_constraint(terms, Layout((0, 1, 2, 3, 4)))
    terms, dqkv2, old_h, old_g = lax.optimization_barrier((terms, dqkv2, h2, g2))
    terms = swap(terms, NEAR)
    base_h = jnp.where(mine, old_h, hidden_in[0])
    base_g = jnp.where(mine, old_g, cotangent[0])
    dnorm2 = norm_terms(dqkv2, w)

    mixed3 = mixed3.astype(BF)
    tile = add(jnp.where(core == 0, mixed3, dnorm2), from_core(jnp.where(core == 0, dnorm2, mixed3)))
    tile = add(tile, from_pair(tile, 1))
    pair = from_pair(tile, 3)

    part = sum_terms(terms)
    shards = swap(part, "zp")

    tile, pair, _ = lax.optimization_barrier((tile, pair, part))
    tile = add(tile, pair)
    other = from_core(tile)
    flags = jnp.stack([core, mine.astype(jnp.int32)])
    hidden_out, grad_in = last_step(flags, tile, other, base_h, base_g, h1, inv2, gain)
    shards, hidden_out, grad_in = lax.optimization_barrier((shards, hidden_out, grad_in))
    grad_qkv = jnp.sum(shards[:, :3].astype(F32), 0)
    grad_out = jnp.sum(shards[:, 3].astype(F32), 0).T
    return (hidden_out[None], grad_in[None], grad_qkv, grad_out)


def solution(mesh):
    grid = Mesh(mesh.devices.reshape(NP, 2, NN // 2, CTX // 2, 2), ("zp", "zq", "y") + CONTEXT)
    dp = ("zp", "zq", "y")
    in_specs = (
        P(dp, CONTEXT, None),
        P(dp, CONTEXT, None),
        P(dp, None),
        P(None, dp, CONTEXT),
        P(CONTEXT, dp),
        P(),
    )
    out_specs = (
        P(dp, CONTEXT, None),
        P(dp, CONTEXT, None),
        P(None, dp, CONTEXT),
        P(CONTEXT, dp),
    )
    return jax.shard_map(
        on_device, mesh=grid, in_specs=in_specs, out_specs=out_specs, check_vma=False
    )
```

```python
import jax
import jax.numpy as jnp
from jax import lax
from jax.experimental import pallas as pl
from jax.experimental.layout import Layout, with_layout_constraint
from jax.experimental.pallas import tpu as pltpu
from jax.sharding import Mesh, PartitionSpec as P

HD = 128
TILE = 128
D = 2048
CTX = 8
NP = 8
NN = 8
NEAR = ("zq", "y")
CHUNK = TILE // CTX
SCALE = HD**-0.5
CONTEXT = ("x", "core")
BF = jnp.bfloat16
F32 = jnp.float32


def swap(x, axis):
    return lax.all_to_all(x, axis, 0, 0)


def spread(x, axis, size):
    return swap(jnp.broadcast_to(x[None], (size,) + x.shape), axis)


def dot(a, b, dims):
    return lax.dot_general(a, b, (dims, ((), ())), preferred_element_type=F32)


def add(a, b):
    return (a.astype(F32) + b.astype(F32)).astype(BF)


def from_core(x):
    return lax.ppermute(x, "core", [(0, 1), (1, 0)])


def from_pair(x, bit):
    return lax.ppermute(x, "x", [(i, i ^ bit) for i in range(CTX // 2)])


def norm_chunk(x32, gain):
    inv = lax.rsqrt(jnp.mean(x32 * x32, -1, keepdims=True) + 1e-06)
    return inv, (x32 * inv * gain).astype(BF)


def all_rows(chunk):
    return lax.all_gather(chunk, CONTEXT, tiled=True)


def sum_chunk(terms):
    return jnp.sum(swap(terms.astype(BF).reshape(CTX, CHUNK, D), CONTEXT).astype(F32), 0)


def forward(rows, w):
    q = dot(rows, w[0], ((1,), (0,))).astype(BF)
    k = dot(rows, w[1], ((1,), (0,))).astype(BF)
    v = dot(rows, w[2], ((1,), (0,))).astype(BF)
    pos = jnp.arange(TILE)
    scores = dot(q, k, ((1,), (1,))) * SCALE
    scores = jnp.where(pos[None, :] <= pos[:, None], scores, -1e30)
    expo = jnp.exp(scores - jnp.max(scores, -1, keepdims=True))
    prob = expo / jnp.sum(expo, -1, keepdims=True)
    probb = prob.astype(BF)
    attn = dot(probb, v, ((1,), (0,))).astype(BF)
    mixed = dot(attn, w[3], ((1,), (1,)))
    return mixed, (rows, q, k, v, prob, probb, attn)


def backward(dy, keep, w):
    rows, q, k, v, prob, probb, attn = keep
    dattn = dot(dy, w[3], ((1,), (0,))).astype(BF)
    delta = jnp.sum(dattn.astype(F32) * attn.astype(F32), -1, keepdims=True)
    dprob = dot(dattn, v, ((1,), (1,)))
    dscore = (prob * (dprob - delta) * SCALE).astype(BF)
    dq = dot(dscore, k, ((1,), (0,))).astype(BF)
    dk = dot(dscore, q, ((0,), (0,))).astype(BF)
    dv = dot(probb, dattn, ((0,), (0,))).astype(BF)
    return dq, dk, dv


def norm_terms(dqkv, w):
    dq, dk, dv = dqkv
    total = dot(dq, w[0], ((1,), (1,))) + dot(dk, w[1], ((1,), (1,))) + dot(dv, w[2], ((1,), (1,)))
    return total.astype(BF)


def norm_grad(e, x32, inv, gain):
    u = e * gain
    return inv * u - x32 * inv**3 * jnp.mean(x32 * u, -1, keepdims=True)


def first_kernel(h, g, w_qkv, w_out, sent, shards, tile_in, qkv_in, out_in, sems, out_sems):
    weights = [
        pltpu.make_async_copy(w_qkv, qkv_in, sems.at[0]),
        pltpu.make_async_copy(w_out, out_in, sems.at[1]),
    ]
    for copy in weights:
        copy.start()
    core = lax.axis_index("core")
    for i, tile in enumerate((g, h)):

        @pl.when(core == i)
        def _(i=i, tile=tile):
            copy = pltpu.make_async_copy(tile, tile_in, sems.at[2 + i])
            copy.start()
            copy.wait()

    parts = [pltpu.make_async_copy(tile_in, sent, sems.at[4])]
    parts[0].start()
    for copy in weights:
        copy.wait()
    for i in range(NP):
        for k, part in enumerate((qkv_in, out_in)):
            place = shards.at[i, pl.ds(0, 3)] if k == 0 else shards.at[i, 3]
            parts.append(pltpu.make_async_copy(part, place, out_sems.at[i, k]))
            parts[-1].start()
    for part in parts:
        part.wait()


def first_step(h, g, w_qkv, w_out):
    return pl.pallas_call(
        first_kernel,
        in_specs=[pl.BlockSpec(memory_space=pl.ANY)] * 4,
        out_specs=[pl.BlockSpec(memory_space=pl.ANY)] * 2,
        out_shape=[
            jax.ShapeDtypeStruct((TILE, D), BF),
            jax.ShapeDtypeStruct((NP, 4, 32, HD), BF),
        ],
        scratch_shapes=[
            pltpu.VMEM((TILE, D), BF),
            pltpu.VMEM((3, 32, HD), BF),
            pltpu.VMEM((32, HD), BF),
            pltpu.SemaphoreType.DMA((5,)),
            pltpu.SemaphoreType.DMA((NP, 2)),
        ],
        compiler_params=pltpu.CompilerParams(vmem_limit_bytes=60 * 2**20),
    )(h, g, w_qkv, w_out)


def sum_kernel(terms, out):
    total = terms[0].astype(F32)
    for i in range(1, NN):
        total = total + terms[i].astype(F32)
    out[...] = total.astype(BF)


def sum_terms(terms):
    return pl.pallas_call(
        sum_kernel,
        out_shape=jax.ShapeDtypeStruct((NP, 4, 32, HD), BF),
        compiler_params=pltpu.CompilerParams(vmem_limit_bytes=16 * 2**20),
    )(terms)


def last_kernel(flags, tile, other, base_h, base_g, h1, inv, gain, out_h, out_g):
    first, mine = flags[0] == 0, flags[1] == 1
    a, b = tile[...].astype(F32), other[...].astype(F32)
    old_h, old_g = base_h[...], base_g[...]
    new_h = (old_h.astype(F32) + jnp.where(first, a, b)).astype(BF)
    dx = norm_grad(jnp.where(first, b, a), h1[...].astype(F32), inv[...], gain[...])
    new_g = (old_g.astype(F32) + dx).astype(BF)
    out_h[...] = jnp.where(mine, new_h, old_h)
    out_g[...] = jnp.where(mine, new_g, old_g)


def last_step(flags, tile, other, base_h, base_g, h1, inv, gain):
    steps = 4
    rows = pl.BlockSpec((TILE // steps, D), lambda i: (i, 0))
    return pl.pallas_call(
        last_kernel,
        grid=(steps,),
        in_specs=[pl.BlockSpec(memory_space=pltpu.SMEM)]
        + [rows] * 5
        + [pl.BlockSpec((TILE // steps, 1), lambda i: (i, 0)), pl.BlockSpec((1, D), lambda i: (0, 0))],
        out_specs=[rows, rows],
        out_shape=[jax.ShapeDtypeStruct((TILE, D), BF)] * 2,
        compiler_params=pltpu.CompilerParams(vmem_limit_bytes=16 * 2**20),
    )(flags, tile, other, base_h, base_g, h1, inv, gain.reshape(1, D))


def on_device(hidden_in, cotangent, tile_depth, w_qkv, w_out, gain):
    me = lax.axis_index("x") * 2 + lax.axis_index("core")
    depth = tile_depth[0]
    live3 = jnp.any(depth >= 3)
    mine = lax.dynamic_index_in_dim(depth, me, 0, keepdims=False) >= 2

    def chunk(tile):
        return lax.dynamic_index_in_dim(tile.reshape(CTX, CHUNK, D), me, 0, keepdims=False)

    tokens = ((0,), (0,))
    core = lax.axis_index("core")
    none = jnp.zeros_like(hidden_in[0])
    sent, shards = first_step(hidden_in[0], cotangent[0], w_qkv, w_out.T)
    near_mine = lax.dynamic_index_in_dim(depth, me + 1 - 2 * core, 0, keepdims=False) >= 2
    kept = jnp.where(mine, jnp.where(core == 0, hidden_in[0], cotangent[0]), none)
    tile = jnp.where(near_mine, from_core(sent), kept)
    tile = tile + from_pair(tile, 1)

    near = swap(shards, "zp")
    near, tile = lax.optimization_barrier((near, tile))
    w = spread(near, NEAR, NN).transpose(2, 1, 0, 3, 4).reshape(4, D, HD)
    tile = tile + from_pair(tile, 3)
    other = from_core(tile)
    h1, g3 = jnp.where(core == 0, tile, other), jnp.where(core == 0, other, tile)
    dy3 = jnp.where(live3, g3, jnp.zeros_like(g3))
    h1, g3, dy3 = lax.optimization_barrier((h1, g3, dy3))

    x1 = h1.astype(F32)
    inv2, rows2 = norm_chunk(x1, gain)
    mixed2, keep2 = forward(rows2, w)
    attn2 = keep2[-1]
    h2c = (chunk(h1).astype(F32) + sum_chunk(mixed2)).astype(BF)
    h2 = all_rows(h2c)

    h2, dy3 = lax.optimization_barrier((h2, dy3))
    x2 = h2.astype(F32)
    inv3, normed3 = norm_chunk(x2, gain)
    rows3 = jnp.where(live3, normed3, jnp.zeros_like(normed3))
    rows3 = lax.optimization_barrier(rows3)
    mixed3, keep3 = forward(rows3, w)
    dqkv3 = backward(dy3, keep3, w)
    dnorm3 = norm_terms(dqkv3, w)
    x2c = chunk(h2).astype(F32)
    inv3c, _ = norm_chunk(x2c, gain)
    g2c = chunk(g3).astype(F32) + norm_grad(sum_chunk(dnorm3), x2c, inv3c, gain)
    g2 = all_rows(g2c.astype(BF))

    dqkv2 = backward(g2, keep2, w)

    def product(left3, right3, left2, right2):
        both = dot(jnp.concatenate([left3, left2], 0), jnp.concatenate([right3, right2], 0), tokens)
        return both.astype(BF).reshape(NP, NN, 32, HD)

    terms = [product(rows3, d3, rows2, d2) for d3, d2 in zip(dqkv3, dqkv2)]
    terms.append(product(dy3, keep3[-1], g2, attn2))
    terms = jnp.stack(terms, 2).transpose(1, 0, 2, 3, 4)
    terms = with_layout_constraint(terms, Layout((0, 1, 2, 3, 4)))
    terms, dqkv2, old_h, old_g = lax.optimization_barrier((terms, dqkv2, h2, g2))
    terms = swap(terms, NEAR)
    base_h = jnp.where(mine, old_h, hidden_in[0])
    base_g = jnp.where(mine, old_g, cotangent[0])
    dnorm2 = norm_terms(dqkv2, w)

    mixed3 = mixed3.astype(BF)
    tile = add(jnp.where(core == 0, mixed3, dnorm2), from_core(jnp.where(core == 0, dnorm2, mixed3)))
    tile = add(tile, from_pair(tile, 1))
    pair = from_pair(tile, 3)

    part = sum_terms(terms)
    shards = swap(part, "zp")

    tile, pair, _ = lax.optimization_barrier((tile, pair, part))
    tile = add(tile, pair)
    other = from_core(tile)
    flags = jnp.stack([core, mine.astype(jnp.int32)])
    hidden_out, grad_in = last_step(flags, tile, other, base_h, base_g, h1, inv2, gain)
    shards, hidden_out, grad_in = lax.optimization_barrier((shards, hidden_out, grad_in))
    grad_qkv = jnp.sum(shards[:, :3].astype(F32), 0)
    grad_out = jnp.sum(shards[:, 3].astype(F32), 0).T
    return (hidden_out[None], grad_in[None], grad_qkv, grad_out)


def solution(mesh):
    grid = Mesh(mesh.devices.reshape(NP, 2, NN // 2, CTX // 2, 2), ("zp", "zq", "y") + CONTEXT)
    dp = ("zp", "zq", "y")
    in_specs = (
        P(dp, CONTEXT, None),
        P(dp, CONTEXT, None),
        P(dp, None),
        P(None, dp, CONTEXT),
        P(CONTEXT, dp),
        P(),
    )
    out_specs = (
        P(dp, CONTEXT, None),
        P(dp, CONTEXT, None),
        P(None, dp, CONTEXT),
        P(CONTEXT, dp),
    )
    return jax.shard_map(
        on_device, mesh=grid, in_specs=in_specs, out_specs=out_specs, check_vma=False
    )
```

```python
import jax
import jax.numpy as jnp
from jax import lax
from jax.experimental import pallas as pl
from jax.experimental.layout import Layout, with_layout_constraint
from jax.experimental.pallas import tpu as pltpu
from jax.sharding import Mesh, PartitionSpec as P

HD = 128
TILE = 128
D = 2048
CTX = 8
NP = 8
NN = 8
NEAR = ("zq", "y")
CHUNK = TILE // CTX
SCALE = HD**-0.5
CONTEXT = ("x", "core")
BF = jnp.bfloat16
F32 = jnp.float32


def swap(x, axis):
    return lax.all_to_all(x, axis, 0, 0)


def spread(x, axis, size):
    return swap(jnp.broadcast_to(x[None], (size,) + x.shape), axis)


def dot(a, b, dims):
    return lax.dot_general(a, b, (dims, ((), ())), preferred_element_type=F32)


def add(a, b):
    return (a.astype(F32) + b.astype(F32)).astype(BF)


def from_core(x):
    return lax.ppermute(x, "core", [(0, 1), (1, 0)])


def from_pair(x, bit):
    return lax.ppermute(x, "x", [(i, i ^ bit) for i in range(CTX // 2)])


def norm_chunk(x32, gain):
    inv = lax.rsqrt(jnp.mean(x32 * x32, -1, keepdims=True) + 1e-06)
    return inv, (x32 * inv * gain).astype(BF)


def all_rows(chunk):
    return lax.all_gather(chunk, CONTEXT, tiled=True)


def sum_chunk(terms):
    return jnp.sum(swap(terms.astype(BF).reshape(CTX, CHUNK, D), CONTEXT).astype(F32), 0)


def forward(rows, w):
    q = dot(rows, w[0], ((1,), (0,))).astype(BF)
    k = dot(rows, w[1], ((1,), (0,))).astype(BF)
    v = dot(rows, w[2], ((1,), (0,))).astype(BF)
    pos = jnp.arange(TILE)
    scores = dot(q, k, ((1,), (1,))) * SCALE
    scores = jnp.where(pos[None, :] <= pos[:, None], scores, -1e30)
    expo = jnp.exp(scores - jnp.max(scores, -1, keepdims=True))
    prob = expo / jnp.sum(expo, -1, keepdims=True)
    probb = prob.astype(BF)
    attn = dot(probb, v, ((1,), (0,))).astype(BF)
    mixed = dot(attn, w[3], ((1,), (1,)))
    return mixed, (rows, q, k, v, prob, probb, attn)


def backward(dy, keep, w):
    rows, q, k, v, prob, probb, attn = keep
    dattn = dot(dy, w[3], ((1,), (0,))).astype(BF)
    delta = jnp.sum(dattn.astype(F32) * attn.astype(F32), -1, keepdims=True)
    dprob = dot(dattn, v, ((1,), (1,)))
    dscore = (prob * (dprob - delta) * SCALE).astype(BF)
    dq = dot(dscore, k, ((1,), (0,))).astype(BF)
    dk = dot(dscore, q, ((0,), (0,))).astype(BF)
    dv = dot(probb, dattn, ((0,), (0,))).astype(BF)
    return dq, dk, dv


def norm_terms(dqkv, w):
    dq, dk, dv = dqkv
    total = dot(dq, w[0], ((1,), (1,))) + dot(dk, w[1], ((1,), (1,))) + dot(dv, w[2], ((1,), (1,)))
    return total.astype(BF)


def norm_grad(e, x32, inv, gain):
    u = e * gain
    return inv * u - x32 * inv**3 * jnp.mean(x32 * u, -1, keepdims=True)


def first_kernel(h, g, w_qkv, w_out, sent, shards, tile_in, qkv_in, out_in, sems, out_sems):
    weights = [
        pltpu.make_async_copy(w_qkv, qkv_in, sems.at[0]),
        pltpu.make_async_copy(w_out, out_in, sems.at[1]),
    ]
    for copy in weights:
        copy.start()
    core = lax.axis_index("core")
    for i, tile in enumerate((g, h)):

        @pl.when(core == i)
        def _(i=i, tile=tile):
            copy = pltpu.make_async_copy(tile, tile_in, sems.at[2 + i])
            copy.start()
            copy.wait()

    parts = [pltpu.make_async_copy(tile_in, sent, sems.at[4])]
    parts[0].start()
    for copy in weights:
        copy.wait()
    for i in range(NP):
        for k, part in enumerate((qkv_in, out_in)):
            place = shards.at[i, pl.ds(0, 3)] if k == 0 else shards.at[i, 3]
            parts.append(pltpu.make_async_copy(part, place, out_sems.at[i, k]))
            parts[-1].start()
    for part in parts:
        part.wait()


def first_step(h, g, w_qkv, w_out):
    return pl.pallas_call(
        first_kernel,
        in_specs=[pl.BlockSpec(memory_space=pl.ANY)] * 4,
        out_specs=[pl.BlockSpec(memory_space=pl.ANY)] * 2,
        out_shape=[
            jax.ShapeDtypeStruct((TILE, D), BF),
            jax.ShapeDtypeStruct((NP, 4, 32, HD), BF),
        ],
        scratch_shapes=[
            pltpu.VMEM((TILE, D), BF),
            pltpu.VMEM((3, 32, HD), BF),
            pltpu.VMEM((32, HD), BF),
            pltpu.SemaphoreType.DMA((5,)),
            pltpu.SemaphoreType.DMA((NP, 2)),
        ],
        compiler_params=pltpu.CompilerParams(vmem_limit_bytes=60 * 2**20),
    )(h, g, w_qkv, w_out)


def copies_kernel(near, out, block, sems):
    for t in range(4):
        block[t] = near[:, t]
    parts = [pltpu.make_async_copy(block, out.at[i], sems.at[i]) for i in range(NN)]
    for part in parts:
        part.start()
    for part in parts:
        part.wait()


def copies(near):
    return pl.pallas_call(
        copies_kernel,
        in_specs=[pl.BlockSpec(memory_space=pltpu.VMEM)],
        out_specs=pl.BlockSpec(memory_space=pl.ANY),
        out_shape=jax.ShapeDtypeStruct((NN, 4, NP, 32, HD), BF),
        scratch_shapes=[pltpu.VMEM((4, NP, 32, HD), BF), pltpu.SemaphoreType.DMA((NN,))],
        compiler_params=pltpu.CompilerParams(vmem_limit_bytes=16 * 2**20),
    )(near)


def sum_kernel(terms, out):
    total = terms[0].astype(F32)
    for i in range(1, NN):
        total = total + terms[i].astype(F32)
    out[...] = total.astype(BF)


def sum_terms(terms):
    return pl.pallas_call(
        sum_kernel,
        out_shape=jax.ShapeDtypeStruct((NP, 4, 32, HD), BF),
        compiler_params=pltpu.CompilerParams(vmem_limit_bytes=16 * 2**20),
    )(terms)


def last_kernel(flags, tile, other, base_h, base_g, h1, inv, gain, out_h, out_g):
    first, mine = flags[0] == 0, flags[1] == 1
    a, b = tile[...].astype(F32), other[...].astype(F32)
    old_h, old_g = base_h[...], base_g[...]
    new_h = (old_h.astype(F32) + jnp.where(first, a, b)).astype(BF)
    dx = norm_grad(jnp.where(first, b, a), h1[...].astype(F32), inv[...], gain[...])
    new_g = (old_g.astype(F32) + dx).astype(BF)
    out_h[...] = jnp.where(mine, new_h, old_h)
    out_g[...] = jnp.where(mine, new_g, old_g)


def last_step(flags, tile, other, base_h, base_g, h1, inv, gain):
    steps = 4
    rows = pl.BlockSpec((TILE // steps, D), lambda i: (i, 0))
    return pl.pallas_call(
        last_kernel,
        grid=(steps,),
        in_specs=[pl.BlockSpec(memory_space=pltpu.SMEM)]
        + [rows] * 5
        + [pl.BlockSpec((TILE // steps, 1), lambda i: (i, 0)), pl.BlockSpec((1, D), lambda i: (0, 0))],
        out_specs=[rows, rows],
        out_shape=[jax.ShapeDtypeStruct((TILE, D), BF)] * 2,
        compiler_params=pltpu.CompilerParams(vmem_limit_bytes=16 * 2**20),
    )(flags, tile, other, base_h, base_g, h1, inv, gain.reshape(1, D))


def on_device(hidden_in, cotangent, tile_depth, w_qkv, w_out, gain):
    me = lax.axis_index("x") * 2 + lax.axis_index("core")
    depth = tile_depth[0]
    live3 = jnp.any(depth >= 3)
    mine = lax.dynamic_index_in_dim(depth, me, 0, keepdims=False) >= 2

    def chunk(tile):
        return lax.dynamic_index_in_dim(tile.reshape(CTX, CHUNK, D), me, 0, keepdims=False)

    tokens = ((0,), (0,))
    core = lax.axis_index("core")
    none = jnp.zeros_like(hidden_in[0])
    sent, shards = first_step(hidden_in[0], cotangent[0], w_qkv, w_out.T)
    near_mine = lax.dynamic_index_in_dim(depth, me + 1 - 2 * core, 0, keepdims=False) >= 2
    kept = jnp.where(mine, jnp.where(core == 0, hidden_in[0], cotangent[0]), none)
    tile = jnp.where(near_mine, from_core(sent), kept)
    tile = tile + from_pair(tile, 1)

    near = swap(shards, "zp")
    near, tile = lax.optimization_barrier((near, tile))
    w = swap(copies(near).transpose(0, 2, 1, 3, 4), NEAR).transpose(2, 1, 0, 3, 4).reshape(4, D, HD)
    tile = tile + from_pair(tile, 3)
    other = from_core(tile)
    h1, g3 = jnp.where(core == 0, tile, other), jnp.where(core == 0, other, tile)
    dy3 = jnp.where(live3, g3, jnp.zeros_like(g3))
    h1, g3, dy3 = lax.optimization_barrier((h1, g3, dy3))

    x1 = h1.astype(F32)
    inv2, rows2 = norm_chunk(x1, gain)
    mixed2, keep2 = forward(rows2, w)
    attn2 = keep2[-1]
    h2c = (chunk(h1).astype(F32) + sum_chunk(mixed2)).astype(BF)
    h2 = all_rows(h2c)

    h2, dy3 = lax.optimization_barrier((h2, dy3))
    x2 = h2.astype(F32)
    inv3, normed3 = norm_chunk(x2, gain)
    rows3 = jnp.where(live3, normed3, jnp.zeros_like(normed3))
    rows3 = lax.optimization_barrier(rows3)
    mixed3, keep3 = forward(rows3, w)
    dqkv3 = backward(dy3, keep3, w)
    dnorm3 = norm_terms(dqkv3, w)
    x2c = chunk(h2).astype(F32)
    inv3c, _ = norm_chunk(x2c, gain)
    g2c = chunk(g3).astype(F32) + norm_grad(sum_chunk(dnorm3), x2c, inv3c, gain)
    g2 = all_rows(g2c.astype(BF))

    dqkv2 = backward(g2, keep2, w)

    def product(left3, right3, left2, right2):
        both = dot(jnp.concatenate([left3, left2], 0), jnp.concatenate([right3, right2], 0), tokens)
        return both.astype(BF).reshape(NP, NN, 32, HD)

    terms = [product(rows3, d3, rows2, d2) for d3, d2 in zip(dqkv3, dqkv2)]
    terms.append(product(dy3, keep3[-1], g2, attn2))
    terms = jnp.stack(terms, 2).transpose(1, 0, 2, 3, 4)
    terms = with_layout_constraint(terms, Layout((0, 1, 2, 3, 4)))
    terms, dqkv2, old_h, old_g = lax.optimization_barrier((terms, dqkv2, h2, g2))
    terms = swap(terms, NEAR)
    base_h = jnp.where(mine, old_h, hidden_in[0])
    base_g = jnp.where(mine, old_g, cotangent[0])
    dnorm2 = norm_terms(dqkv2, w)

    mixed3 = mixed3.astype(BF)
    tile = add(jnp.where(core == 0, mixed3, dnorm2), from_core(jnp.where(core == 0, dnorm2, mixed3)))
    tile = add(tile, from_pair(tile, 1))
    pair = from_pair(tile, 3)

    part = sum_terms(terms)
    shards = swap(part, "zp")

    tile, pair, _ = lax.optimization_barrier((tile, pair, part))
    tile = add(tile, pair)
    other = from_core(tile)
    flags = jnp.stack([core, mine.astype(jnp.int32)])
    hidden_out, grad_in = last_step(flags, tile, other, base_h, base_g, h1, inv2, gain)
    shards, hidden_out, grad_in = lax.optimization_barrier((shards, hidden_out, grad_in))
    grad_qkv = jnp.sum(shards[:, :3].astype(F32), 0)
    grad_out = jnp.sum(shards[:, 3].astype(F32), 0).T
    return (hidden_out[None], grad_in[None], grad_qkv, grad_out)


def solution(mesh):
    grid = Mesh(mesh.devices.reshape(NP, 2, NN // 2, CTX // 2, 2), ("zp", "zq", "y") + CONTEXT)
    dp = ("zp", "zq", "y")
    in_specs = (
        P(dp, CONTEXT, None),
        P(dp, CONTEXT, None),
        P(dp, None),
        P(None, dp, CONTEXT),
        P(CONTEXT, dp),
        P(),
    )
    out_specs = (
        P(dp, CONTEXT, None),
        P(dp, CONTEXT, None),
        P(None, dp, CONTEXT),
        P(CONTEXT, dp),
    )
    return jax.shard_map(
        on_device, mesh=grid, in_specs=in_specs, out_specs=out_specs, check_vma=False
    )
```

```python
import jax
import jax.numpy as jnp
from jax import lax
from jax.experimental import pallas as pl
from jax.experimental.pallas import tpu as pltpu
from jax.sharding import Mesh, PartitionSpec as P

HD = 128
TILE = 128
D = 2048
CTX = 8
NP = 8
NN = 8
NEAR = ("zq", "y")
CHUNK = TILE // CTX
SCALE = HD**-0.5
CONTEXT = ("x", "core")
BF = jnp.bfloat16
F32 = jnp.float32


def swap(x, axis):
    return lax.all_to_all(x, axis, 0, 0)


def spread(x, axis, size):
    return swap(jnp.broadcast_to(x[None], (size,) + x.shape), axis)


def dot(a, b, dims):
    return lax.dot_general(a, b, (dims, ((), ())), preferred_element_type=F32)


def add(a, b):
    return (a.astype(F32) + b.astype(F32)).astype(BF)


def from_core(x):
    return lax.ppermute(x, "core", [(0, 1), (1, 0)])


def from_pair(x, bit):
    return lax.ppermute(x, "x", [(i, i ^ bit) for i in range(CTX // 2)])


def norm_chunk(x32, gain):
    inv = lax.rsqrt(jnp.mean(x32 * x32, -1, keepdims=True) + 1e-06)
    return inv, (x32 * inv * gain).astype(BF)


def all_rows(chunk):
    return lax.all_gather(chunk, CONTEXT, tiled=True)


def sum_chunk(terms):
    return jnp.sum(swap(terms.astype(BF).reshape(CTX, CHUNK, D), CONTEXT).astype(F32), 0)


def forward(rows, w):
    q = dot(rows, w[0], ((1,), (0,))).astype(BF)
    k = dot(rows, w[1], ((1,), (0,))).astype(BF)
    v = dot(rows, w[2], ((1,), (0,))).astype(BF)
    pos = jnp.arange(TILE)
    scores = dot(q, k, ((1,), (1,))) * SCALE
    scores = jnp.where(pos[None, :] <= pos[:, None], scores, -1e30)
    expo = jnp.exp(scores - jnp.max(scores, -1, keepdims=True))
    prob = expo / jnp.sum(expo, -1, keepdims=True)
    probb = prob.astype(BF)
    attn = dot(probb, v, ((1,), (0,))).astype(BF)
    mixed = dot(attn, w[3], ((1,), (1,)))
    return mixed, (rows, q, k, v, prob, probb, attn)


def backward(dy, keep, w):
    rows, q, k, v, prob, probb, attn = keep
    dattn = dot(dy, w[3], ((1,), (0,))).astype(BF)
    delta = jnp.sum(dattn.astype(F32) * attn.astype(F32), -1, keepdims=True)
    dprob = dot(dattn, v, ((1,), (1,)))
    dscore = (prob * (dprob - delta) * SCALE).astype(BF)
    dq = dot(dscore, k, ((1,), (0,))).astype(BF)
    dk = dot(dscore, q, ((0,), (0,))).astype(BF)
    dv = dot(probb, dattn, ((0,), (0,))).astype(BF)
    return dq, dk, dv


def norm_terms(dqkv, w):
    dq, dk, dv = dqkv
    total = dot(dq, w[0], ((1,), (1,))) + dot(dk, w[1], ((1,), (1,))) + dot(dv, w[2], ((1,), (1,)))
    return total.astype(BF)


def norm_grad(e, x32, inv, gain):
    u = e * gain
    return inv * u - x32 * inv**3 * jnp.mean(x32 * u, -1, keepdims=True)


def first_kernel(h, g, w_qkv, w_out, sent, shards, tile_in, qkv_in, out_in, sems, out_sems):
    weights = [
        pltpu.make_async_copy(w_qkv, qkv_in, sems.at[0]),
        pltpu.make_async_copy(w_out, out_in, sems.at[1]),
    ]
    for copy in weights:
        copy.start()
    core = lax.axis_index("core")
    for i, tile in enumerate((g, h)):

        @pl.when(core == i)
        def _(i=i, tile=tile):
            copy = pltpu.make_async_copy(tile, tile_in, sems.at[2 + i])
            copy.start()
            copy.wait()

    parts = [pltpu.make_async_copy(tile_in, sent, sems.at[4])]
    parts[0].start()
    for copy in weights:
        copy.wait()
    for i in range(NP):
        for k, part in enumerate((qkv_in, out_in)):
            place = shards.at[i, pl.ds(0, 3)] if k == 0 else shards.at[i, 3]
            parts.append(pltpu.make_async_copy(part, place, out_sems.at[i, k]))
            parts[-1].start()
    for part in parts:
        part.wait()


def first_step(h, g, w_qkv, w_out):
    return pl.pallas_call(
        first_kernel,
        in_specs=[pl.BlockSpec(memory_space=pl.ANY)] * 4,
        out_specs=[pl.BlockSpec(memory_space=pl.ANY)] * 2,
        out_shape=[
            jax.ShapeDtypeStruct((TILE, D), BF),
            jax.ShapeDtypeStruct((NP, 4, 32, HD), BF),
        ],
        scratch_shapes=[
            pltpu.VMEM((TILE, D), BF),
            pltpu.VMEM((3, 32, HD), BF),
            pltpu.VMEM((32, HD), BF),
            pltpu.SemaphoreType.DMA((5,)),
            pltpu.SemaphoreType.DMA((NP, 2)),
        ],
        compiler_params=pltpu.CompilerParams(vmem_limit_bytes=60 * 2**20),
    )(h, g, w_qkv, w_out)


def copies_kernel(near, out, block, sems):
    for t in range(4):
        block[t] = near[:, t]
    parts = [pltpu.make_async_copy(block, out.at[i], sems.at[i]) for i in range(NN)]
    for part in parts:
        part.start()
    for part in parts:
        part.wait()


def copies(near):
    return pl.pallas_call(
        copies_kernel,
        in_specs=[pl.BlockSpec(memory_space=pltpu.VMEM)],
        out_specs=pl.BlockSpec(memory_space=pl.ANY),
        out_shape=jax.ShapeDtypeStruct((NN, 4, NP, 32, HD), BF),
        scratch_shapes=[pltpu.VMEM((4, NP, 32, HD), BF), pltpu.SemaphoreType.DMA((NN,))],
        compiler_params=pltpu.CompilerParams(vmem_limit_bytes=16 * 2**20),
    )(near)


def order_kernel(q, k, v, o, out):
    for t, part in enumerate((q, k, v, o)):
        for n in range(NN):
            out[n, :, t] = part[:, n]


def in_order(q, k, v, o):
    return pl.pallas_call(
        order_kernel,
        out_shape=jax.ShapeDtypeStruct((NN, NP, 4, 32, HD), BF),
        compiler_params=pltpu.CompilerParams(vmem_limit_bytes=16 * 2**20),
    )(q, k, v, o)


def sum_kernel(terms, out):
    total = terms[0].astype(F32)
    for i in range(1, NN):
        total = total + terms[i].astype(F32)
    out[...] = total.astype(BF)


def sum_terms(terms):
    return pl.pallas_call(
        sum_kernel,
        out_shape=jax.ShapeDtypeStruct((NP, 4, 32, HD), BF),
        compiler_params=pltpu.CompilerParams(vmem_limit_bytes=16 * 2**20),
    )(terms)


def last_kernel(flags, tile, other, base_h, base_g, h1, inv, gain, out_h, out_g):
    first, mine = flags[0] == 0, flags[1] == 1
    a, b = tile[...].astype(F32), other[...].astype(F32)
    old_h, old_g = base_h[...], base_g[...]
    new_h = (old_h.astype(F32) + jnp.where(first, a, b)).astype(BF)
    dx = norm_grad(jnp.where(first, b, a), h1[...].astype(F32), inv[...], gain[...])
    new_g = (old_g.astype(F32) + dx).astype(BF)
    out_h[...] = jnp.where(mine, new_h, old_h)
    out_g[...] = jnp.where(mine, new_g, old_g)


def last_step(flags, tile, other, base_h, base_g, h1, inv, gain):
    steps = 4
    rows = pl.BlockSpec((TILE // steps, D), lambda i: (i, 0))
    return pl.pallas_call(
        last_kernel,
        grid=(steps,),
        in_specs=[pl.BlockSpec(memory_space=pltpu.SMEM)]
        + [rows] * 5
        + [pl.BlockSpec((TILE // steps, 1), lambda i: (i, 0)), pl.BlockSpec((1, D), lambda i: (0, 0))],
        out_specs=[rows, rows],
        out_shape=[jax.ShapeDtypeStruct((TILE, D), BF)] * 2,
        compiler_params=pltpu.CompilerParams(vmem_limit_bytes=16 * 2**20),
    )(flags, tile, other, base_h, base_g, h1, inv, gain.reshape(1, D))


def on_device(hidden_in, cotangent, tile_depth, w_qkv, w_out, gain):
    me = lax.axis_index("x") * 2 + lax.axis_index("core")
    depth = tile_depth[0]
    live3 = jnp.any(depth >= 3)
    mine = lax.dynamic_index_in_dim(depth, me, 0, keepdims=False) >= 2

    def chunk(tile):
        return lax.dynamic_index_in_dim(tile.reshape(CTX, CHUNK, D), me, 0, keepdims=False)

    tokens = ((0,), (0,))
    core = lax.axis_index("core")
    none = jnp.zeros_like(hidden_in[0])
    sent, shards = first_step(hidden_in[0], cotangent[0], w_qkv, w_out.T)
    near_mine = lax.dynamic_index_in_dim(depth, me + 1 - 2 * core, 0, keepdims=False) >= 2
    kept = jnp.where(mine, jnp.where(core == 0, hidden_in[0], cotangent[0]), none)
    tile = jnp.where(near_mine, from_core(sent), kept)
    tile = tile + from_pair(tile, 1)

    near = swap(shards, "zp")
    near, tile = lax.optimization_barrier((near, tile))
    w = swap(copies(near).transpose(0, 2, 1, 3, 4), NEAR).transpose(2, 1, 0, 3, 4).reshape(4, D, HD)
    tile = tile + from_pair(tile, 3)
    other = from_core(tile)
    h1, g3 = jnp.where(core == 0, tile, other), jnp.where(core == 0, other, tile)
    dy3 = jnp.where(live3, g3, jnp.zeros_like(g3))
    h1, g3, dy3 = lax.optimization_barrier((h1, g3, dy3))

    x1 = h1.astype(F32)
    inv2, rows2 = norm_chunk(x1, gain)
    mixed2, keep2 = forward(rows2, w)
    attn2 = keep2[-1]
    h2c = (chunk(h1).astype(F32) + sum_chunk(mixed2)).astype(BF)
    h2 = all_rows(h2c)

    h2, dy3 = lax.optimization_barrier((h2, dy3))
    x2 = h2.astype(F32)
    inv3, normed3 = norm_chunk(x2, gain)
    rows3 = jnp.where(live3, normed3, jnp.zeros_like(normed3))
    rows3 = lax.optimization_barrier(rows3)
    mixed3, keep3 = forward(rows3, w)
    dqkv3 = backward(dy3, keep3, w)
    dnorm3 = norm_terms(dqkv3, w)
    x2c = chunk(h2).astype(F32)
    inv3c, _ = norm_chunk(x2c, gain)
    g2c = chunk(g3).astype(F32) + norm_grad(sum_chunk(dnorm3), x2c, inv3c, gain)
    g2 = all_rows(g2c.astype(BF))

    dqkv2 = backward(g2, keep2, w)

    def product(left3, right3, left2, right2):
        both = dot(jnp.concatenate([left3, left2], 0), jnp.concatenate([right3, right2], 0), tokens)
        return both.astype(BF).reshape(NP, NN, 32, HD)

    terms = [product(rows3, d3, rows2, d2) for d3, d2 in zip(dqkv3, dqkv2)]
    terms.append(product(dy3, keep3[-1], g2, attn2))
    terms = in_order(*terms)
    terms, dqkv2, old_h, old_g = lax.optimization_barrier((terms, dqkv2, h2, g2))
    terms = swap(terms, NEAR)
    base_h = jnp.where(mine, old_h, hidden_in[0])
    base_g = jnp.where(mine, old_g, cotangent[0])
    dnorm2 = norm_terms(dqkv2, w)

    mixed3 = mixed3.astype(BF)
    tile = add(jnp.where(core == 0, mixed3, dnorm2), from_core(jnp.where(core == 0, dnorm2, mixed3)))
    tile = add(tile, from_pair(tile, 1))
    pair = from_pair(tile, 3)

    part = sum_terms(terms)
    shards = swap(part, "zp")

    tile, pair, _ = lax.optimization_barrier((tile, pair, part))
    tile = add(tile, pair)
    other = from_core(tile)
    flags = jnp.stack([core, mine.astype(jnp.int32)])
    hidden_out, grad_in = last_step(flags, tile, other, base_h, base_g, h1, inv2, gain)
    shards, hidden_out, grad_in = lax.optimization_barrier((shards, hidden_out, grad_in))
    grad_qkv = jnp.sum(shards[:, :3].astype(F32), 0)
    grad_out = jnp.sum(shards[:, 3].astype(F32), 0).T
    return (hidden_out[None], grad_in[None], grad_qkv, grad_out)


def solution(mesh):
    grid = Mesh(mesh.devices.reshape(NP, 2, NN // 2, CTX // 2, 2), ("zp", "zq", "y") + CONTEXT)
    dp = ("zp", "zq", "y")
    in_specs = (
        P(dp, CONTEXT, None),
        P(dp, CONTEXT, None),
        P(dp, None),
        P(None, dp, CONTEXT),
        P(CONTEXT, dp),
        P(),
    )
    out_specs = (
        P(dp, CONTEXT, None),
        P(dp, CONTEXT, None),
        P(None, dp, CONTEXT),
        P(CONTEXT, dp),
    )
    return jax.shard_map(
        on_device, mesh=grid, in_specs=in_specs, out_specs=out_specs, check_vma=False
    )
```
